512 devices in a mesh: comp: 128 (over z, y, core), col: 4 (over x).
Axes of the slice: x: 4, y: 8, z: 8, core: 2. Of those that a mesh axis runs over, the one named last changes fastest.
Arguments:
- operators: bfloat16 [1024, 512, 1024], P('comp', 'col'), may hold values from -0.1875 to 0.1875
- excitations: bfloat16 [1024, 1024, 512], P('comp', None, 'col'), may hold values from -6 to 6
- comp_scale: float32 [1024], P('comp'), may hold values from 0.2 to 5
- live_count: int32 [128], P('comp'), may hold values from 1 to 8, 512 in all
- port_of: int32 [1024, 64], P('comp', 'col'), may hold values from 0 to 65535, as said below
Outputs:
- port_basis: bfloat16 [65536, 8, 256], P(('comp', 'col'))
- upper_factor: float32 [512, 512], replicated
The draws below stay inside these ranges and needn't reach their ends.
Inputs may be any that keep to these rules, and one draw needn't show every extreme that they name: `live_count`: 8 on some comp device in every draw; the entries sum to 512. `port_of`: a permutation of the port block positions; position p belongs to comp device p // 512 and col device (p // 128) % 4, and a block stays on its col device; of the blocks one device holds, exactly 2 go to each of 64 comp devices.
All inputs are finite; a program needn't handle non-finite values.
Results may differ from the reference program's by a relative error of at most 0.0085.
Values may be sent and summed in bfloat16 or wider, within the bound.
A program may use at most 64 MiB of HBM per device.

```python
import math
import jax
import jax.numpy as jnp
import numpy as np
from jax import lax

RC = 512
PIN = 1024
COLS = 512
MODES = 256
BROWS = 8
COMP_DEV = 8
SLOTS = 1024
ALLROWS = 524288
PORT_BLOCKS = 65536
N_COMP = 128
N_COL = 4


def draw_port_of(key, part):
    key = jax.random.fold_in(key, 7)
    per_col = RC // BROWS // N_COL
    per_dev = COMP_DEV * per_col
    capacity = 2 * per_dev // N_COMP
    first_key, second_key, third_key = jax.random.split(key, 3)
    relabel = jax.random.permutation(first_key, N_COMP)
    inverse = jnp.argsort(relabel)
    shifts = jax.vmap(lambda sub_key: jax.random.permutation(sub_key, N_COMP)[:per_dev // capacity])(jax.random.split(second_key, N_COL))
    source = jnp.arange(N_COMP)[:, None, None]
    column = jnp.arange(N_COL)[None, :, None]
    local_index = jnp.arange(per_dev)[None, None, :]
    shift_now = shifts[column, local_index // capacity]
    target = inverse[(relabel[source] + shift_now) % N_COMP]
    shuffle = jax.vmap(lambda sub_key: jax.random.permutation(sub_key, per_dev))(jax.random.split(third_key, N_COMP * N_COL)).reshape(N_COMP, N_COL, per_dev)
    place_in = shuffle[target, column, local_index]
    position = (target * N_COL + column) * per_dev + place_in
    position = position.reshape(N_COMP, N_COL, COMP_DEV, per_col).transpose(0, 2, 1, 3).reshape(N_COMP * COMP_DEV, N_COL * per_col)
    return position.astype(jnp.int32)


def level_of(rng, shape, cuts, smallest, largest):
    level = 1.0
    for dim, parts in cuts:
        draws = jax.random.uniform(jax.random.fold_in(jax.random.fold_in(rng, 6), dim), (parts,), jnp.float32, smallest / len(cuts), largest / len(cuts))
        level = level * jnp.repeat(jnp.exp(draws), shape[dim] // parts).reshape((-1,) + (1,) * (len(shape) - 1 - dim))
    return level


def profile(count, total, bound, lean):
    portions = [(1 << 20) // math.isqrt(grade ** lean) + 1 for grade in range(2, count + 1)]
    rest, counts = total - bound - (count - 1), [1] * (count - 1)
    while rest > 0:
        candidates = [i for i in range(count - 1) if counts[i] < bound]
        pool, budget = sum([portions[i] for i in candidates]), rest
        for i in candidates:
            more = min(bound - counts[i], max(1, budget * portions[i] // pool), rest)
            counts[i] = counts[i] + more
            rest = rest - more
    return np.array([bound] + counts)


def ragged_sizes(own_key, amount, total, bound, skew):
    if amount == 2:
        one = jax.random.randint(own_key, (), max(1, total - bound), min(bound, total - 1) + 1)
        return jnp.stack([one, total - one])
    tallies = jnp.asarray(profile(amount, total, bound, skew), jnp.int32)
    twos = (amount - 1) // 2
    giver, taker = tallies[1:1 + 2 * twos:2], tallies[2:2 + 2 * twos:2]
    margin = jnp.minimum(giver - 1, bound - taker)
    shifted = jax.random.randint(jax.random.fold_in(own_key, 1), (twos,), 0, 1 << 20) % (margin + 1)
    tallies = tallies.at[1:1 + 2 * twos:2].set(giver - shifted).at[2:2 + 2 * twos:2].set(taker + shifted)
    return tallies[jax.random.permutation(jax.random.fold_in(own_key, 2), amount)]


def gaussian(own_key, extent, spread, bound, cuts=(), kind=jnp.bfloat16):
    array = spread * jax.random.normal(own_key, extent, jnp.float32)
    if cuts:
        array = array * level_of(own_key, extent, cuts, -0.22, 0.18)
    return jnp.clip(array, -bound, bound).astype(kind)


def setup_inputs(seed: int = 0) -> dict:
    key_of = jax.random.split(jax.random.key(seed), 6)
    return {
        "operators": gaussian(key_of[0], (SLOTS, RC, PIN), PIN ** -0.5, 0.1875, ((0, 128), (1, 4))),
        "excitations": gaussian(key_of[1], (SLOTS, PIN, COLS), 1.0, 6.0, ((0, 128), (2, 4))),
        "comp_scale": jnp.clip(jnp.exp(math.log(5.0) - 3.218876 * jax.random.uniform(key_of[2], (SLOTS,), jnp.float32) ** level_of(key_of[2], (SLOTS,), ((0, 128),), -0.2, 0.2)), 0.2, 5.0),
        "live_count": ragged_sizes(key_of[3], N_COMP, N_COMP * COMP_DEV // 2, COMP_DEV, 2).astype(jnp.int32),
        "port_of": draw_port_of(jax.random.fold_in(key_of[5], 71), 0),
    }


def reference(operators, excitations, comp_scale, live_count, port_of):
    slot_index = jnp.arange(SLOTS, dtype=jnp.int32)
    owning = slot_index // COMP_DEV
    within = slot_index % COMP_DEV
    living = (within < live_count[owning]).astype(jnp.float32)
    weights = comp_scale * living

    def apply_one(items):
        operator_one, excite_one, weight_one = items
        product = jnp.dot(operator_one.astype(jnp.float32), excite_one.astype(jnp.float32), preferred_element_type=jnp.float32)
        return (weight_one * product).astype(jnp.bfloat16)
    snapshot = lax.map(apply_one, (operators, excitations, weights)).reshape(SLOTS * RC, COLS)
    gram_sum = lax.dot_general(snapshot.astype(jnp.float32), snapshot.astype(jnp.float32), (((0,), (0,)), ((), ())), preferred_element_type=jnp.float32)
    normed = gram_sum / ALLROWS
    upper_factor = jnp.linalg.cholesky(normed).T
    leading = snapshot[:, :MODES].astype(jnp.float32)
    head_block = upper_factor[:MODES, :MODES]
    solved = jax.scipy.linalg.solve_triangular(head_block, leading.T, trans=1, lower=False)
    modes = solved.T.astype(jnp.bfloat16).reshape(PORT_BLOCKS, BROWS, MODES)
    port_basis = jnp.zeros((PORT_BLOCKS, BROWS, MODES), jnp.bfloat16).at[port_of.reshape(-1).astype(jnp.int32)].set(modes)
    return (port_basis, upper_factor)
```

```python
import jax
import jax.numpy as jnp
from jax import lax
from jax.experimental import pallas as pl
from jax.experimental.pallas import tpu as pltpu
from jax.sharding import PartitionSpec as P

MESH = pl.DeviceIdType.MESH
NX, NY, NZ, NT = 4, 8, 8, 16
F32, BF16, I32 = jnp.float32, jnp.bfloat16, jnp.int32
FIRST = [(0, 0), (0, 1), (0, 2), (0, 3), (1, 1), (1, 2), (1, 3)]
SECOND = [(2, 2), (2, 3), (3, 3)]


def iota(shape, dim):
    return lax.broadcasted_iota(I32, shape, dim)


def gather_kernel(ops, exc, scale, live, ports, gram_out, lead_out,
                  A, E, W, lead, P_pack, P_un, pmine, pz, ptile, pall,
                  PA, PB, RA1, RA2, RB1, RB2,
                  g0, g1, r0c, r1c, s0, s1, rz0, ry1, t0, t1, ry0, rz1, u0, u1, rx0, rx1,
                  ay0, az1, az0, ay1, f0, f1,
                  local_sem, s_ops, r_ops, s_exc, r_exc, s_pz, r_pz, s_py, r_py, s_ld, r_ld,
                  s_core, r_core, s_red, r_red, s_x, r_x, s_rel, r_rel):
    comp, x = lax.axis_index("comp"), lax.axis_index("col")
    z, y, core = comp // 16, (comp // 2) % 8, comp % 2
    t = y * 2 + core

    def at(xx=None, yy=None, zz=None, cc=None):
        xx, yy, zz, cc = (x if xx is None else xx, y if yy is None else yy, z if zz is None else zz, core if cc is None else cc)
        return ((zz * 8 + yy) * 2 + cc, xx)

    def at_t(tt):
        return (z * 16 + tt, x)

    started = []

    def send(src, dst, ss, rs, to):
        copy = pltpu.make_async_remote_copy(src_ref=src, dst_ref=dst, send_sem=ss, recv_sem=rs, device_id=to, device_id_type=MESH)
        copy.start()
        started.append(copy)

    def arrived(dst, ss, rs, frm):
        pltpu.make_async_remote_copy(src_ref=dst, dst_ref=dst, send_sem=ss, recv_sem=rs, device_id=frm, device_id_type=MESH).wait_recv()

    xs = [(d, lax.rem(x + d, NX), lax.rem(x + NX - d, NX)) for d in (1, 3, 2)]
    ys = [(d, lax.rem(y + d, NY), lax.rem(y + NY - d, NY)) for d in (4, 3, 5, 2, 6, 1, 7)]
    zs = [(d, lax.rem(z + d, NZ), lax.rem(z + NZ - d, NZ)) for d in (4, 3, 5, 2, 6, 1, 7)]
    ts = [(d, lax.rem(t + d, NT), lax.rem(t + NT - d, NT)) for d in (8, 7, 9, 6, 10, 5, 11, 4, 12, 3, 13, 2, 14, 1, 15)]
    other = 1 - core

    barrier = pltpu.get_barrier_semaphore()
    for _, to, _ in xs:
        pl.semaphore_signal(barrier, inc=1, device_id=at(xx=to), device_id_type=MESH)
    for _, to, _ in zs:
        pl.semaphore_signal(barrier, inc=1, device_id=at(zz=to), device_id_type=MESH)
    for _, to, _ in ts:
        pl.semaphore_signal(barrier, inc=1, device_id=at_t(to), device_id_type=MESH)

    own = []
    for k in range(2):
        own.append(pltpu.make_async_copy(ops.at[2 * x + k], A.at[k, pl.ds(pl.multiple_of(x * 128, 128), 128), :], local_sem.at[k]))
        own.append(pltpu.make_async_copy(exc.at[2 * x + k], E.at[k, :, pl.ds(pl.multiple_of(x * 128, 128), 128)], local_sem.at[2 + k]))
    for copy in own:
        copy.start()
    pl.semaphore_wait(barrier, 3 + 7 + 15)

    rows_me = pl.ds(pl.multiple_of(x * 128, 128), 128)
    for k in range(2):
        for d, to, _ in xs:
            send(ops.at[2 * to + k], A.at[k, rows_me, :], s_ops.at[k, d - 1], r_ops.at[k, d - 1], at(xx=to))
            send(exc.at[2 * to + k], E.at[k, :, rows_me], s_exc.at[k, d - 1], r_exc.at[k, d - 1], at(xx=to))

    p_local = ports[...]
    pmine[...] = jnp.broadcast_to(p_local, (8, 128)).astype(F32)
    pz[z] = pmine[...]
    for d, to, _ in zs:
        send(pmine, pz.at[z], s_pz.at[d - 1], r_pz.at[d - 1], at(zz=to))
    target = p_local // 512
    target_all = jnp.broadcast_to(target.astype(F32), (128, 128))
    target_col = target_all.T
    earlier = (target_col == target_all) & (iota((128, 128), 0) < iota((128, 128), 1))
    rank = jnp.sum(earlier.astype(F32), axis=0, keepdims=True)
    base = jnp.broadcast_to(target.astype(F32) * 2 + rank, (8, 128)).astype(BF16)
    spread = (iota((128, 1024), 1) // 8 == iota((128, 1024), 0)).astype(BF16)
    key = jnp.dot(base, spread, preferred_element_type=F32)[0:1, :].astype(I32) * 8 + iota((1, 1024), 1) % 8

    def fill_pack(n, carry):
        P_pack[pl.ds(pl.multiple_of(n * 128, 128), 128), :] = (iota((128, 1024), 0) + n * 128 == key).astype(F32).astype(BF16)
        return carry
    lax.fori_loop(0, 16, fill_pack, 0)

    for d, _, frm in zs:
        arrived(pz.at[frm], s_pz.at[d - 1], r_pz.at[d - 1], at(zz=frm))
    tile = jnp.concatenate([pz[n, 0:1, :] for n in range(8)], axis=0)
    ptile[...] = tile
    pall[t] = tile
    for d, to, _ in ts:
        send(ptile, pall.at[t], s_py.at[d - 1], r_py.at[d - 1], at_t(to))
    for d, _, frm in ts:
        arrived(pall.at[frm], s_py.at[d - 1], r_py.at[d - 1], at_t(frm))
    every = pall[...].reshape(128, 128).astype(I32)
    mine = jnp.where(every // 512 == comp, every % 128 + 1, 0).astype(F32).T
    is_mine = (mine > 0.5)
    below = (iota((128, 128), 1) < iota((128, 128), 0)).astype(BF16)
    order = jnp.dot(below, is_mine.astype(F32).astype(BF16), preferred_element_type=F32)
    zero = jnp.zeros((128, 128), F32)
    first = jnp.sum(jnp.where(is_mine & (order < 0.5), mine, zero), axis=0, keepdims=True)
    second = jnp.sum(jnp.where(is_mine & (order > 0.5), mine, zero), axis=0, keepdims=True)
    both = jnp.concatenate([first, second, jnp.zeros((6, 128), F32)], axis=0).astype(BF16)
    lane = iota((128, 2048), 1) // 16
    widen = ((lane % 16) * 8 + lane // 16 == iota((128, 2048), 0)).astype(F32).astype(BF16)
    wide = jnp.dot(both, widen, preferred_element_type=F32)
    which = (iota((1, 2048), 1) // 8) % 2
    place = jnp.where(which == 0, wide[0:1, :], wide[1:2, :]).astype(I32) * 8 - 8 + iota((1, 2048), 1) % 8

    def fill_un(n, carry):
        P_un[pl.ds(pl.multiple_of(n * 128, 128), 128), :] = (iota((128, 2048), 0) + n * 128 == place).astype(F32).astype(BF16)
        return carry
    lax.fori_loop(0, 8, fill_un, 0)

    for copy in own:
        copy.wait()
    gram = jnp.zeros((512, 512), F32)
    for k in range(2):
        for d, _, frm in xs:
            there = pl.ds(pl.multiple_of(frm * 128, 128), 128)
            arrived(A.at[k, there, :], s_ops.at[k, d - 1], r_ops.at[k, d - 1], at(xx=frm))
            arrived(E.at[k, :, there], s_exc.at[k, d - 1], r_exc.at[k, d - 1], at(xx=frm))
        slot = 2 * x + k
        alive = jnp.minimum(jnp.maximum(live[0] - slot, 0), 1).astype(F32)
        weight = scale[slot] * alive

        def rows(n, carry):
            where = pl.ds(pl.multiple_of(n * 128, 128), 128)
            product = jnp.dot(A[k, where, :], E[k], preferred_element_type=F32)
            W[k, where, :] = (product * weight).astype(BF16)
            return carry
        lax.fori_loop(0, 4, rows, 0)
        for d, to, _ in xs:
            send(W.at[k, pl.ds(pl.multiple_of(to * 128, 128), 128), pl.ds(0, 256)], lead.at[2 * x + k], s_ld.at[k, d - 1], r_ld.at[k, d - 1], at(xx=to))
        lead[2 * x + k] = W[k, rows_me, 0:256]

    def gram_block(r, c):
        out = lax.dot_general(W[0, :, r * 128:(r + 1) * 128], W[0, :, c * 128:(c + 1) * 128], (((0,), (0,)), ((), ())), preferred_element_type=F32)
        return out + lax.dot_general(W[1, :, r * 128:(r + 1) * 128], W[1, :, c * 128:(c + 1) * 128], (((0,), (0,)), ((), ())), preferred_element_type=F32)

    for n, (r, c) in enumerate(FIRST):
        g0[n * 128:(n + 1) * 128, :] = gram_block(r, c)
    for n, (r, c) in enumerate(SECOND):
        g1[n * 128:(n + 1) * 128, :] = gram_block(r, c)

    send(g0.at[pl.ds(pl.multiple_of(other * 448, 64), 448), :], r0c, s_core.at[0], r_core.at[0], at(cc=other))
    send(g1.at[pl.ds(pl.multiple_of(other * 192, 64), 192), :], r1c, s_core.at[1], r_core.at[1], at(cc=other))
    arrived(r0c, s_core.at[0], r_core.at[0], at(cc=other))
    s0[...] = g0[pl.ds(pl.multiple_of(core * 448, 64), 448), :] + r0c[...]
    for d, to, _ in zs:
        send(s0.at[pl.ds(pl.multiple_of(to * 56, 8), 56), :], rz0.at[z], s_red.at[0, d - 1], r_red.at[0, d - 1], at(zz=to))
    arrived(r1c, s_core.at[1], r_core.at[1], at(cc=other))
    s1[...] = g1[pl.ds(pl.multiple_of(core * 192, 64), 192), :] + r1c[...]
    for d, to, _ in ys:
        send(s1.at[pl.ds(pl.multiple_of(to * 24, 8), 24), :], ry1.at[y], s_red.at[1, d - 1], r_red.at[1, d - 1], at(yy=to))
    rz0[z] = s0[pl.ds(pl.multiple_of(z * 56, 8), 56), :]
    ry1[y] = s1[pl.ds(pl.multiple_of(y * 24, 8), 24), :]

    for k in range(2):
        for d, _, frm in xs:
            arrived(lead.at[2 * frm + k], s_ld.at[k, d - 1], r_ld.at[k, d - 1], at(xx=frm))

    def pack(n, carry):
        packed = jnp.dot(P_pack[pl.ds(pl.multiple_of(n * 256, 256), 256), :], lead[...].reshape(1024, 256), preferred_element_type=F32).astype(BF16)
        PA[pl.ds(n * 16, 16)] = packed[:, 0:128].reshape(16, 16, 128)
        PB[n] = packed[:, 128:256].reshape(16, 16, 128)
        return carry
    lax.fori_loop(0, 8, pack, 0)
    for (d, to, _) in zs:
        send(PA.at[pl.ds(to * 16, 16)], RA1.at[z], s_rel.at[0, d - 1], r_rel.at[0, d - 1], at(zz=to))
    for (d, to, _) in ts:
        send(PB.at[:, to], RB1.at[t], s_rel.at[1, d - 1], r_rel.at[1, d - 1], at_t(to))
    RA1[z] = PA[pl.ds(z * 16, 16)]
    RB1[t] = PB[:, t]

    for d, _, frm in zs:
        arrived(rz0.at[frm], s_red.at[0, d - 1], r_red.at[0, d - 1], at(zz=frm))
    t0[0:56, :] = sum([rz0[n] for n in range(1, 8)], rz0[0])
    t0[56:64, :] = jnp.zeros((8, 128), F32)
    for d, to, _ in ys:
        send(t0.at[pl.ds(pl.multiple_of(to * 8, 8), 8), :], ry0.at[y], s_red.at[2, d - 1], r_red.at[2, d - 1], at(yy=to))
    ry0[y] = t0[pl.ds(pl.multiple_of(y * 8, 8), 8), :]
    for d, _, frm in ys:
        arrived(ry1.at[frm], s_red.at[1, d - 1], r_red.at[1, d - 1], at(yy=frm))
    t1[0:24, :] = sum([ry1[n] for n in range(1, 8)], ry1[0])
    t1[24:64, :] = jnp.zeros((40, 128), F32)
    for d, to, _ in zs:
        send(t1.at[pl.ds(pl.multiple_of(to * 8, 8), 8), :], rz1.at[z], s_red.at[3, d - 1], r_red.at[3, d - 1], at(zz=to))
    rz1[z] = t1[pl.ds(pl.multiple_of(z * 8, 8), 8), :]

    for d, _, frm in ys:
        arrived(ry0.at[frm], s_red.at[2, d - 1], r_red.at[2, d - 1], at(yy=frm))
    u0[...] = sum([ry0[n] for n in range(1, 8)], ry0[0])
    for d, to, _ in xs:
        send(u0, rx0.at[x], s_x.at[0, d - 1], r_x.at[0, d - 1], at(xx=to))
    rx0[x] = u0[...]
    for d, _, frm in zs:
        arrived(rz1.at[frm], s_red.at[3, d - 1], r_red.at[3, d - 1], at(zz=frm))
    u1[...] = sum([rz1[n] for n in range(1, 8)], rz1[0])
    for d, to, _ in xs:
        send(u1, rx1.at[x], s_x.at[1, d - 1], r_x.at[1, d - 1], at(xx=to))
    rx1[x] = u1[...]

    for d, _, frm in xs:
        arrived(rx0.at[frm], s_x.at[0, d - 1], r_x.at[0, d - 1], at(xx=frm))
    ay0[pl.ds(pl.multiple_of(y * 8, 8), 8), :] = (rx0[0] + rx0[1]) + (rx0[2] + rx0[3])
    mine0 = ay0.at[pl.ds(pl.multiple_of(y * 8, 8), 8), :]
    for d, to, _ in ys:
        send(mine0, mine0, s_red.at[4, d - 1], r_red.at[4, d - 1], at(yy=to))
    for d, _, frm in xs:
        arrived(rx1.at[frm], s_x.at[1, d - 1], r_x.at[1, d - 1], at(xx=frm))
    az1[pl.ds(pl.multiple_of(z * 8, 8), 8), :] = (rx1[0] + rx1[1]) + (rx1[2] + rx1[3])
    mine1 = az1.at[pl.ds(pl.multiple_of(z * 8, 8), 8), :]
    for d, to, _ in zs:
        send(mine1, mine1, s_red.at[5, d - 1], r_red.at[5, d - 1], at(zz=to))

    for d, _, frm in ys:
        arrived(ay0.at[pl.ds(pl.multiple_of(frm * 8, 8), 8), :], s_red.at[4, d - 1], r_red.at[4, d - 1], at(yy=frm))
    az0[z] = ay0[0:56, :]
    for d, to, _ in zs:
        send(ay0.at[0:56, :], az0.at[z], s_red.at[6, d - 1], r_red.at[6, d - 1], at(zz=to))
    for d, _, frm in zs:
        arrived(az1.at[pl.ds(pl.multiple_of(frm * 8, 8), 8), :], s_red.at[5, d - 1], r_red.at[5, d - 1], at(zz=frm))
    ay1[y] = az1[0:24, :]
    for d, to, _ in ys:
        send(az1.at[0:24, :], ay1.at[y], s_red.at[7, d - 1], r_red.at[7, d - 1], at(yy=to))

    for d, _, frm in zs:
        arrived(RA1.at[frm], s_rel.at[0, d - 1], r_rel.at[0, d - 1], at(zz=frm))
    for d, to, _ in ts:
        send(RA1.at[:, to], RA2.at[:, t], s_rel.at[2, d - 1], r_rel.at[2, d - 1], at_t(to))
    RA2[:, t] = RA1[:, t]
    for d, _, frm in ts:
        arrived(RB1.at[frm], s_rel.at[1, d - 1], r_rel.at[1, d - 1], at_t(frm))
    for d, to, _ in zs:
        send(RB1.at[:, to], RB2.at[z], s_rel.at[3, d - 1], r_rel.at[3, d - 1], at(zz=to))
    RB2[z] = RB1[:, z]

    for d, _, frm in zs:
        arrived(az0.at[frm], s_red.at[6, d - 1], r_red.at[6, d - 1], at(zz=frm))
    f0[core] = az0[...].reshape(448, 128)
    mine_f0 = f0.at[core]
    send(mine_f0, mine_f0, s_core.at[2], r_core.at[2], at(cc=other))
    for d, _, frm in ys:
        arrived(ay1.at[frm], s_red.at[7, d - 1], r_red.at[7, d - 1], at(yy=frm))
    f1[core] = ay1[...].reshape(192, 128)
    mine_f1 = f1.at[core]
    send(mine_f1, mine_f1, s_core.at[3], r_core.at[3], at(cc=other))

    for d, _, frm in ts:
        arrived(RA2.at[:, frm], s_rel.at[2, d - 1], r_rel.at[2, d - 1], at_t(frm))
    for d, _, frm in zs:
        arrived(RB2.at[frm], s_rel.at[3, d - 1], r_rel.at[3, d - 1], at(zz=frm))

    def unpack(n, carry):
        where = pl.ds(pl.multiple_of(n * 256, 256), 256)
        pick = P_un[where, :]
        lead_out[where, 0:128] = jnp.dot(pick, RA2[...].reshape(2048, 128), preferred_element_type=F32).astype(BF16)
        lead_out[where, 128:256] = jnp.dot(pick, RB2[...].reshape(2048, 128), preferred_element_type=F32).astype(BF16)
        return carry
    lax.fori_loop(0, 4, unpack, 0)

    arrived(f0.at[other], s_core.at[2], r_core.at[2], at(cc=other))
    arrived(f1.at[other], s_core.at[3], r_core.at[3], at(cc=other))
    gram_out[0:7] = f0[...].reshape(7, 128, 128)
    gram_out[7:10] = f1[...].reshape(3, 128, 128)
    for copy in started:
        copy.wait_send()


def gather_and_sum(ops, exc, scale, live, ports):
    D = pltpu.SemaphoreType.DMA
    vm = pltpu.VMEM
    V, H, S = (pl.BlockSpec(memory_space=m) for m in (pltpu.VMEM, pl.ANY, pltpu.SMEM))
    scratch = [
        vm((2, 512, 1024), BF16), vm((2, 1024, 512), BF16), vm((2, 512, 512), BF16), vm((8, 128, 256), BF16),
        vm((2048, 1024), BF16), vm((1024, 2048), BF16),
        vm((8, 128), F32), vm((8, 8, 128), F32), vm((8, 128), F32), vm((16, 8, 128), F32),
        vm((128, 16, 128), BF16), vm((8, 16, 16, 128), BF16),
        vm((8, 16, 16, 128), BF16), vm((8, 16, 16, 128), BF16), vm((16, 8, 16, 128), BF16), vm((8, 16, 16, 128), BF16),
        vm((896, 128), F32), vm((384, 128), F32), vm((448, 128), F32), vm((192, 128), F32),
        vm((448, 128), F32), vm((192, 128), F32),
        vm((8, 56, 128), F32), vm((8, 24, 128), F32), vm((64, 128), F32), vm((64, 128), F32),
        vm((8, 8, 128), F32), vm((8, 8, 128), F32), vm((8, 128), F32), vm((8, 128), F32),
        vm((4, 8, 128), F32), vm((4, 8, 128), F32),
        vm((64, 128), F32), vm((64, 128), F32), vm((8, 56, 128), F32), vm((8, 24, 128), F32),
        vm((2, 448, 128), F32), vm((2, 192, 128), F32),
        D((4,)), D((2, 3)), D((2, 3)), D((2, 3)), D((2, 3)), D((7,)), D((7,)), D((15,)), D((15,)), D((2, 3)), D((2, 3)),
        D((4,)), D((4,)), D((8, 7)), D((8, 7)), D((2, 3)), D((2, 3)), D((4, 15)), D((4, 15)),
    ]
    return pl.pallas_call(
        gather_kernel,
        out_shape=(jax.ShapeDtypeStruct((10, 128, 128), F32), jax.ShapeDtypeStruct((1024, 256), BF16)),
        in_specs=[H, H, S, S, V], out_specs=(V, V),
        scratch_shapes=scratch,
        compiler_params=pltpu.CompilerParams(collective_id=0, has_side_effects=True, vmem_limit_bytes=48 << 20),
        name="gather_and_sum",
    )(ops, exc, scale, live, ports)


HI = lax.Precision.HIGHEST

def dot_hi(a, b, ta=False):
    dims = (((0,), (0,)), ((), ())) if ta else (((1,), (0,)), ((), ()))
    return lax.dot_general(a, b, dims, precision=HI, preferred_element_type=jnp.float32)

def factor_block(S):
    sub = lax.broadcasted_iota(jnp.int32, (8, 128), 0)
    lane = lax.broadcasted_iota(jnp.int32, (8, 128), 1)
    S = list(S)
    T = [(lane == sub + 8 * i).astype(jnp.float32) for i in range(16)]
    for j in range(16):
        B = {i: [jnp.broadcast_to(S[i][:, 8 * j + k:8 * j + k + 1], (8, 128)) for k in range(8)] for i in range(j, 16)}
        scale = jnp.zeros((8, 128), jnp.float32)
        for k in range(8):
            piv = B[j][k][k:k + 1, :]
            inv = 1.0 / piv
            scale = jnp.where(sub == k, lax.rsqrt(piv), scale)
            prow, qrow = S[j][k:k + 1, :], T[j][k:k + 1, :]
            brow = [B[j][kk][k:k + 1, :] for kk in range(8)]
            for i in range(j, 16):
                m = B[i][k] * inv
                if i == j:
                    m = jnp.where(sub > k, m, 0.0)
                if i > j or k < 7:
                    S[i] = S[i] - m * prow
                    T[i] = T[i] - m * qrow
                    for kk in range(k + 1, 8):
                        B[i][kk] = B[i][kk] - m * brow[kk]
        S[j] = jnp.where(lane >= sub + 8 * j, S[j], 0.0) * scale
        T[j] = T[j] * scale
    return S, T

def k2_body(g_ref, lead_ref, basis_ref, upper_ref, S, T):
    blocks = [(0, 0), (0, 1), (0, 2), (0, 3), (1, 1), (1, 2), (1, 3), (2, 2), (2, 3), (3, 3)]
    inv_rows = 1.0 / 524288
    for n, (r, c) in enumerate(blocks):
        S[r * 128:(r + 1) * 128, c * 128:(c + 1) * 128] = g_ref[n] * inv_rows
    for r in range(4):
        for c in range(r):
            S[r * 128:(r + 1) * 128, c * 128:(c + 1) * 128] = jnp.zeros((128, 128), jnp.float32)

    def step(kb, carry):
        r0 = pl.multiple_of(kb * 128, 128)
        tiles = [S[pl.ds(r0 + 8 * i, 8), pl.ds(r0, 128)] for i in range(16)]
        U, Tt = factor_block(tiles)
        for i in range(16):
            T[kb, 8 * i:8 * i + 8, :] = Tt[i]
        row = dot_hi(T[kb], S[pl.ds(r0, 128), :])
        col = lax.broadcasted_iota(jnp.int32, (128, 512), 1)
        row = jnp.where(col >= r0 + 128, row, 0.0)
        upper_ref[pl.ds(r0, 128), :] = row
        for i in range(16):
            upper_ref[pl.ds(r0 + 8 * i, 8), pl.ds(r0, 128)] = U[i]
        S[...] = S[...] - dot_hi(row, row, ta=True)
        return carry
    lax.fori_loop(0, 4, step, 0)
    t0, t1 = T[0].T, T[1].T
    cross = -dot_hi(t0, dot_hi(upper_ref[0:128, 128:256], t1))
    top = jnp.concatenate([t0, cross], axis=1)
    bot = jnp.concatenate([jnp.zeros((128, 128), jnp.float32), t1], axis=1)
    rinv = jnp.concatenate([top, bot], axis=0)
    hi = rinv.astype(jnp.bfloat16)
    rest = rinv - hi.astype(jnp.float32)
    mid = rest.astype(jnp.bfloat16)
    lo = (rest - mid.astype(jnp.float32)).astype(jnp.bfloat16)
    def modes(n, carry):
        x = lead_ref[pl.ds(pl.multiple_of(n * 256, 256), 256), :]
        y = jnp.dot(x, lo, preferred_element_type=jnp.float32)
        y = y + jnp.dot(x, mid, preferred_element_type=jnp.float32)
        y = y + jnp.dot(x, hi, preferred_element_type=jnp.float32)
        basis_ref[pl.ds(n * 32, 32), :, :] = y.reshape(32, 8, 256).astype(jnp.bfloat16)
        return carry
    lax.fori_loop(0, 4, modes, 0)

def factor_and_modes(gram_blocks, lead):
    V = pl.BlockSpec(memory_space=pltpu.VMEM)
    return pl.pallas_call(
        k2_body,
        out_shape=(jax.ShapeDtypeStruct((128, 8, 256), jnp.bfloat16), jax.ShapeDtypeStruct((512, 512), jnp.float32)),
        in_specs=[V, V], out_specs=(V, V),
        scratch_shapes=[pltpu.VMEM((512, 512), jnp.float32), pltpu.VMEM((4, 128, 128), jnp.float32)],
        compiler_params=pltpu.CompilerParams(vmem_limit_bytes=32 << 20),
        name="factor_modes",
    )(gram_blocks, lead)


def on_device(operators, excitations, comp_scale, live_count, port_of):
    gram_blocks, lead = gather_and_sum(operators, excitations, comp_scale, live_count, port_of.reshape(1, 128))
    return factor_and_modes(gram_blocks, lead)


def solution(mesh):
    placed = (P("comp", "col", None), P("comp", None, "col"), P("comp"), P("comp"), P("comp", "col"))
    return jax.shard_map(on_device, mesh=mesh, in_specs=placed, out_specs=(P(("comp", "col"), None, None), P()), check_vma=False)
```

```python
import jax
import jax.numpy as jnp
from jax import lax
from jax.experimental import pallas as pl
from jax.experimental.pallas import tpu as pltpu
from jax.sharding import PartitionSpec as P

MESH = pl.DeviceIdType.MESH
NX, NY, NZ, NT = 4, 8, 8, 16
F32, BF16, I32 = jnp.float32, jnp.bfloat16, jnp.int32
FIRST = [(0, 0), (0, 1), (0, 2), (0, 3), (1, 1)]
SECOND = [(1, 2), (1, 3), (2, 2), (2, 3), (3, 3)]


CUT_Z, CUT_T = (0, 0, 3, 5, 7), (0, 0, 6, 11, 15)
HI = lax.Precision.HIGHEST


def iota(shape, dim):
    return lax.broadcasted_iota(I32, shape, dim)


def dot_hi(a, b, ta=False):
    dims = (((0,), (0,)), ((), ())) if ta else (((1,), (0,)), ((), ()))
    return lax.dot_general(a, b, dims, precision=HI, preferred_element_type=jnp.float32)

def factor_block(S):
    sub = lax.broadcasted_iota(jnp.int32, (8, 128), 0)
    lane = lax.broadcasted_iota(jnp.int32, (8, 128), 1)
    S = list(S)
    T = [(lane == sub + 8 * i).astype(jnp.float32) for i in range(16)]
    for j in range(16):
        B = {i: [jnp.broadcast_to(S[i][:, 8 * j + k:8 * j + k + 1], (8, 128)) for k in range(8)] for i in range(j, 16)}
        scale = jnp.zeros((8, 128), jnp.float32)
        for k in range(8):
            piv = B[j][k][k:k + 1, :]
            inv = 1.0 / piv
            scale = jnp.where(sub == k, lax.rsqrt(piv), scale)
            prow, qrow = S[j][k:k + 1, :], T[j][k:k + 1, :]
            brow = [B[j][kk][k:k + 1, :] for kk in range(8)]
            for i in range(j, 16):
                m = B[i][k] * inv
                if i == j:
                    m = jnp.where(sub > k, m, 0.0)
                if i > j or k < 7:
                    S[i] = S[i] - m * prow
                    T[i] = T[i] - m * qrow
                    for kk in range(k + 1, 8):
                        B[i][kk] = B[i][kk] - m * brow[kk]
        S[j] = jnp.where(lane >= sub + 8 * j, S[j], 0.0) * scale
        T[j] = T[j] * scale
    return S, T


def factor_rows(S, T, upper, after_first, row_done):
    def step(kb, carry):
        r0 = pl.multiple_of(kb * 128, 128)
        U, inverse = factor_block([S[pl.ds(r0 + 8 * i, 8), pl.ds(r0, 128)] for i in range(16)])
        for i in range(16):
            T[kb, 8 * i:8 * i + 8, :] = inverse[i]
            upper[pl.ds(r0 + 8 * i, 8), pl.ds(r0, 128)] = U[i]
        for n in range(4):
            @pl.when(kb == n)
            def _(n=n):
                edge = (n + 1) * 128
                if n == 0:
                    after_first()
                if n < 3:
                    row = dot_hi(T[n], S[n * 128:edge, edge:])
                    upper[n * 128:edge, edge:] = row
                row_done(n)
                for r in range(n + 1, 4):
                    right = row[:, r * 128 - edge:]
                    S[r * 128:r * 128 + 128, r * 128:] = S[r * 128:r * 128 + 128, r * 128:] - dot_hi(right[:, 0:128], right, ta=True)
        return carry
    lax.fori_loop(0, 4, step, 0)


def finish_kernel(upper_in, pieces_hbm, lead_hbm, basis, upper, passing, pieces, lead, out, sems):
    half = [pl.ds(n * 256, 256) for n in range(4)]
    whole = [pltpu.make_async_copy(upper_in.at[half[n], :], passing.at[half[n], :], sems.at[n]) for n in range(2)]
    copies = [pltpu.make_async_copy(pieces_hbm, pieces, sems.at[2])]
    copies += [pltpu.make_async_copy(lead_hbm.at[half[n], :], lead.at[half[n], :], sems.at[3 + n]) for n in range(4)]
    for copy in copies + whole:
        copy.start()
    back = []
    for n in range(2):
        whole[n].wait()
        back.append(pltpu.make_async_copy(passing.at[half[n], :], upper.at[half[n], :], sems.at[11 + n]))
        back[n].start()
    copies[0].wait()
    for n in range(4):
        copies[1 + n].wait()
        block = lead[half[n], :]
        total = jnp.dot(block, pieces[2], preferred_element_type=F32)
        total = total + jnp.dot(block, pieces[1], preferred_element_type=F32)
        total = total + jnp.dot(block, pieces[0], preferred_element_type=F32)
        out[pl.ds(n * 32, 32)] = total.reshape(32, 8, 256).astype(BF16)
        back.append(pltpu.make_async_copy(out.at[pl.ds(n * 32, 32)], basis.at[pl.ds(n * 32, 32)], sems.at[7 + n]))
        back[2 + n].start()
    for copy in back:
        copy.wait()


def finish(upper, pieces, lead):
    H = pl.BlockSpec(memory_space=pl.ANY)
    return pl.pallas_call(
        finish_kernel,
        out_shape=(jax.ShapeDtypeStruct((128, 8, 256), BF16), jax.ShapeDtypeStruct((512, 512), F32)),
        in_specs=[H] * 3, out_specs=(H, H),
        scratch_shapes=[pltpu.VMEM((512, 512), F32), pltpu.VMEM((3, 256, 256), BF16), pltpu.VMEM((1024, 256), BF16),
                        pltpu.VMEM((128, 8, 256), BF16), pltpu.SemaphoreType.DMA((13,))],
        compiler_params=pltpu.CompilerParams(vmem_limit_bytes=60 << 20),
        name="modes",
    )(upper, pieces, lead)


def fused_kernel(ops, exc, scale_hbm, live_hbm, ports_hbm, upper_hbm, pieces_hbm, lead_hbm,
                 A, E, W, lead, P_pack, P_un, ports, scale, live, pmine, pz, ptile, pall,
                 PA, PB, RA1, RA2, RB1, RB2,
                 S, T, upper, pieces, lead_out, out_sem, g0, g1, r0c, r1c, s0, s1, rz0, ry1, t0, t1, ry0, rz1, u0, u1, rx0, rx1,
                 ay0, az1, az0, ay1, f0, f1,
                 local_sem, s_ops, r_ops, s_exc, r_exc, s_pz, r_pz, s_py, r_py, s_ld, r_ld,
                 s_core, r_core, s_red, r_red, s_x, r_x, s_rel, r_rel):
    comp, x = lax.axis_index("comp"), lax.axis_index("col")
    z, y, core = comp // 16, (comp // 2) % 8, comp % 2
    t = y * 2 + core

    def at(xx=None, yy=None, zz=None, cc=None):
        xx, yy, zz, cc = (x if xx is None else xx, y if yy is None else yy, z if zz is None else zz, core if cc is None else cc)
        return ((zz * 8 + yy) * 2 + cc, xx)

    def at_t(tt):
        return (z * 16 + tt, x)

    started = []

    def send(src, dst, ss, rs, to):
        copy = pltpu.make_async_remote_copy(src_ref=src, dst_ref=dst, send_sem=ss, recv_sem=rs, device_id=to, device_id_type=MESH)
        copy.start()
        started.append(copy)

    def arrived(dst, ss, rs, frm):
        pltpu.make_async_remote_copy(src_ref=dst, dst_ref=dst, send_sem=ss, recv_sem=rs, device_id=frm, device_id_type=MESH).wait_recv()

    xs = [(d, lax.rem(x + d, NX), lax.rem(x + NX - d, NX)) for d in (1, 3, 2)]
    ys = [(d, lax.rem(y + d, NY), lax.rem(y + NY - d, NY)) for d in (4, 3, 5, 2, 6, 1, 7)]
    zs = [(d, lax.rem(z + d, NZ), lax.rem(z + NZ - d, NZ)) for d in (4, 3, 5, 2, 6, 1, 7)]
    ts = [(d, lax.rem(t + d, NT), lax.rem(t + NT - d, NT)) for d in (8, 7, 9, 6, 10, 5, 11, 4, 12, 3, 13, 2, 14, 1, 15)]
    other = 1 - core

    barrier = pltpu.get_barrier_semaphore()
    for _, to, _ in xs:
        pl.semaphore_signal(barrier, inc=1, device_id=at(xx=to), device_id_type=MESH)
    for _, to, _ in zs:
        pl.semaphore_signal(barrier, inc=1, device_id=at(zz=to), device_id_type=MESH)
    for _, to, _ in ts:
        pl.semaphore_signal(barrier, inc=1, device_id=at_t(to), device_id_type=MESH)

    small = [pltpu.make_async_copy(ports_hbm, ports, local_sem.at[4]),
             pltpu.make_async_copy(scale_hbm, scale, local_sem.at[5]),
             pltpu.make_async_copy(live_hbm, live, local_sem.at[6])]
    for copy in small:
        copy.start()
    own = []
    for k in range(2):
        own.append(pltpu.make_async_copy(ops.at[2 * x + k], A.at[k, pl.ds(pl.multiple_of(x * 128, 128), 128), :], local_sem.at[k]))
        own.append(pltpu.make_async_copy(exc.at[2 * x + k], E.at[k, :, pl.ds(pl.multiple_of(x * 128, 128), 128)], local_sem.at[2 + k]))
    for copy in own:
        copy.start()
    pl.semaphore_wait(barrier, 3 + 7 + 15)

    rows_me = pl.ds(pl.multiple_of(x * 128, 128), 128)
    for k in range(2):
        for d, to, _ in xs:
            send(ops.at[2 * to + k], A.at[k, rows_me, :], s_ops.at[k, d - 1], r_ops.at[k, d - 1], at(xx=to))
            send(exc.at[2 * to + k], E.at[k, :, rows_me], s_exc.at[k, d - 1], r_exc.at[k, d - 1], at(xx=to))

    for copy in small:
        copy.wait()
    pick = (iota((16, 128), 1) % 16 == iota((16, 128), 0)).astype(F32).astype(BF16)
    p_high = jnp.dot((ports[...] // 256).astype(F32).astype(BF16), pick, preferred_element_type=F32)
    p_low = jnp.dot((ports[...] % 256).astype(F32).astype(BF16), pick, preferred_element_type=F32)
    p_local = jnp.where(iota((8, 128), 1) // 16 == iota((8, 128), 0), p_high * 256 + p_low, 0.0)
    p_local = jnp.sum(p_local, axis=0, keepdims=True).astype(I32)
    pmine[...] = jnp.broadcast_to(p_local, (8, 128)).astype(F32)
    pz[z] = pmine[...]
    for d, to, _ in zs:
        send(pmine, pz.at[z], s_pz.at[d - 1], r_pz.at[d - 1], at(zz=to))
    target = p_local // 512
    target_all = jnp.broadcast_to(target.astype(F32), (128, 128))
    target_col = target_all.T
    earlier = (target_col == target_all) & (iota((128, 128), 0) < iota((128, 128), 1))
    rank = jnp.sum(earlier.astype(F32), axis=0, keepdims=True)
    base = jnp.broadcast_to(target.astype(F32) * 2 + rank, (8, 128)).astype(BF16)
    spread = (iota((128, 1024), 1) // 8 == iota((128, 1024), 0)).astype(BF16)
    key = jnp.dot(base, spread, preferred_element_type=F32)[0:1, :].astype(I32) * 8 + iota((1, 1024), 1) % 8

    def fill_pack(n, carry):
        P_pack[pl.ds(pl.multiple_of(n * 128, 128), 128), :] = (iota((128, 1024), 0) + n * 128 == key).astype(F32).astype(BF16)
        return carry
    lax.fori_loop(0, 16, fill_pack, 0)

    for d, _, frm in zs:
        arrived(pz.at[frm], s_pz.at[d - 1], r_pz.at[d - 1], at(zz=frm))
    tile = jnp.concatenate([pz[n, 0:1, :] for n in range(8)], axis=0)
    ptile[...] = tile
    pall[t] = tile
    for d, to, _ in ts:
        send(ptile, pall.at[t], s_py.at[d - 1], r_py.at[d - 1], at_t(to))
    for d, _, frm in ts:
        arrived(pall.at[frm], s_py.at[d - 1], r_py.at[d - 1], at_t(frm))
    every = pall[...].reshape(128, 128).astype(I32)
    mine = jnp.where(every // 512 == comp, every % 128 + 1, 0).astype(F32).T
    is_mine = (mine > 0.5)
    below = (iota((128, 128), 1) < iota((128, 128), 0)).astype(BF16)
    order = jnp.dot(below, is_mine.astype(F32).astype(BF16), preferred_element_type=F32)
    zero = jnp.zeros((128, 128), F32)
    first = jnp.sum(jnp.where(is_mine & (order < 0.5), mine, zero), axis=0, keepdims=True)
    second = jnp.sum(jnp.where(is_mine & (order > 0.5), mine, zero), axis=0, keepdims=True)
    both = jnp.concatenate([first, second, jnp.zeros((6, 128), F32)], axis=0).astype(BF16)
    lane = iota((128, 2048), 1) // 16
    widen = ((lane % 16) * 8 + lane // 16 == iota((128, 2048), 0)).astype(F32).astype(BF16)
    wide = jnp.dot(both, widen, preferred_element_type=F32)
    which = (iota((1, 2048), 1) // 8) % 2
    place = jnp.where(which == 0, wide[0:1, :], wide[1:2, :]).astype(I32) * 8 - 8 + iota((1, 2048), 1) % 8

    def fill_un(n, carry):
        P_un[pl.ds(pl.multiple_of(n * 128, 128), 128), :] = (iota((128, 2048), 0) + n * 128 == place).astype(F32).astype(BF16)
        return carry
    lax.fori_loop(0, 8, fill_un, 0)

    def send_leads(k):
        for d, to, _ in xs:
            send(W.at[k, pl.ds(pl.multiple_of(to * 128, 128), 128), pl.ds(0, 256)], lead.at[2 * x + k], s_ld.at[k, d - 1], r_ld.at[k, d - 1], at(xx=to))
        lead[2 * x + k] = W[k, rows_me, 0:256]

    for copy in own:
        copy.wait()
    for k in range(2):
        for d, _, frm in xs:
            there = pl.ds(pl.multiple_of(frm * 128, 128), 128)
            arrived(A.at[k, there, :], s_ops.at[k, d - 1], r_ops.at[k, d - 1], at(xx=frm))
            arrived(E.at[k, :, there], s_exc.at[k, d - 1], r_exc.at[k, d - 1], at(xx=frm))
        slot = 2 * x + k
        alive = jnp.minimum(jnp.maximum(live[0] - slot, 0), 1).astype(F32)
        weight = scale[slot] * alive

        def rows(n, carry):
            where = pl.ds(pl.multiple_of(n * 256, 256), 256)
            product = jnp.dot(A[k, where, :], E[k], preferred_element_type=F32)
            W[k, where, :] = (product * weight).astype(BF16)
            return carry
        lax.fori_loop(0, 2, rows, 0)
        if k == 0:
            send_leads(0)
        for r in range(4):
            out = lax.dot_general(W[k, :, r * 128:(r + 1) * 128], W[k, :, r * 128:], (((0,), (0,)), ((), ())), preferred_element_type=F32)
            for c in range(r, 4):
                g, n = (g0, FIRST.index((r, c))) if (r, c) in FIRST else (g1, SECOND.index((r, c)))
                part = out[:, (c - r) * 128:(c - r + 1) * 128]
                g[n * 128:(n + 1) * 128, :] = part if k == 0 else g[n * 128:(n + 1) * 128, :] + part
            if k == 1 and r == 1:
                send(g0.at[pl.ds(pl.multiple_of(other * 320, 64), 320), :], r0c, s_core.at[0], r_core.at[0], at(cc=other))
    send(g1.at[pl.ds(pl.multiple_of(other * 320, 64), 320), :], r1c, s_core.at[1], r_core.at[1], at(cc=other))
    send_leads(1)
    arrived(r0c, s_core.at[0], r_core.at[0], at(cc=other))
    s0[...] = g0[pl.ds(pl.multiple_of(core * 320, 64), 320), :] + r0c[...]
    for d, to, _ in zs:
        send(s0.at[pl.ds(pl.multiple_of(to * 40, 8), 40), :], rz0.at[z], s_red.at[0, d - 1], r_red.at[0, d - 1], at(zz=to))
    arrived(r1c, s_core.at[1], r_core.at[1], at(cc=other))
    s1[...] = g1[pl.ds(pl.multiple_of(core * 320, 64), 320), :] + r1c[...]
    for d, to, _ in ys:
        send(s1.at[pl.ds(pl.multiple_of(to * 40, 8), 40), :], ry1.at[y], s_red.at[1, d - 1], r_red.at[1, d - 1], at(yy=to))
    rz0[z] = s0[pl.ds(pl.multiple_of(z * 40, 8), 40), :]
    ry1[y] = s1[pl.ds(pl.multiple_of(y * 40, 8), 40), :]

    for k in range(2):
        for d, _, frm in xs:
            arrived(lead.at[2 * frm + k], s_ld.at[k, d - 1], r_ld.at[k, d - 1], at(xx=frm))

    def pack(n, carry):
        packed = jnp.dot(P_pack[pl.ds(pl.multiple_of(n * 256, 256), 256), :], lead[...].reshape(1024, 256), preferred_element_type=F32).astype(BF16)
        PA[pl.ds(n * 16, 16)] = packed[:, 0:128].reshape(16, 16, 128)
        PB[n] = packed[:, 128:256].reshape(16, 16, 128)
        return carry
    lax.fori_loop(0, 8, pack, 0)

    def first_leg(bunch):
        for d, to, _ in zs[CUT_Z[bunch]:CUT_Z[bunch + 1]]:
            send(PA.at[pl.ds(to * 16, 16)], RA1.at[z], s_rel.at[0, d - 1], r_rel.at[0, d - 1], at(zz=to))
        for d, to, _ in ts[CUT_T[bunch]:CUT_T[bunch + 1]]:
            send(PB.at[:, to], RB1.at[t], s_rel.at[1, d - 1], r_rel.at[1, d - 1], at_t(to))

    def second_leg():
        for d, _, frm in zs:
            arrived(RA1.at[frm], s_rel.at[0, d - 1], r_rel.at[0, d - 1], at(zz=frm))
        for d, to, _ in ts:
            send(RA1.at[:, to], RA2.at[:, t], s_rel.at[2, d - 1], r_rel.at[2, d - 1], at_t(to))
        RA2[:, t] = RA1[:, t]
        for d, _, frm in ts:
            arrived(RB1.at[frm], s_rel.at[1, d - 1], r_rel.at[1, d - 1], at_t(frm))
        for d, to, _ in zs:
            send(RB1.at[:, to], RB2.at[z], s_rel.at[3, d - 1], r_rel.at[3, d - 1], at(zz=to))
        RB2[z] = RB1[:, z]

    first_leg(0)
    RA1[z] = PA[pl.ds(z * 16, 16)]
    RB1[t] = PB[:, t]
    for d, _, frm in zs:
        arrived(rz0.at[frm], s_red.at[0, d - 1], r_red.at[0, d - 1], at(zz=frm))
    t0[0:40, :] = sum([rz0[n] for n in range(1, 8)], rz0[0])
    t0[40:64, :] = jnp.zeros((24, 128), F32)
    for d, to, _ in ys:
        send(t0.at[pl.ds(pl.multiple_of(to * 8, 8), 8), :], ry0.at[y], s_red.at[2, d - 1], r_red.at[2, d - 1], at(yy=to))
    ry0[y] = t0[pl.ds(pl.multiple_of(y * 8, 8), 8), :]
    for d, _, frm in ys:
        arrived(ry1.at[frm], s_red.at[1, d - 1], r_red.at[1, d - 1], at(yy=frm))
    t1[0:40, :] = sum([ry1[n] for n in range(1, 8)], ry1[0])
    t1[40:64, :] = jnp.zeros((24, 128), F32)
    for d, to, _ in zs:
        send(t1.at[pl.ds(pl.multiple_of(to * 8, 8), 8), :], rz1.at[z], s_red.at[3, d - 1], r_red.at[3, d - 1], at(zz=to))
    rz1[z] = t1[pl.ds(pl.multiple_of(z * 8, 8), 8), :]

    first_leg(1)
    for d, _, frm in ys:
        arrived(ry0.at[frm], s_red.at[2, d - 1], r_red.at[2, d - 1], at(yy=frm))
    u0[...] = sum([ry0[n] for n in range(1, 8)], ry0[0])
    for d, to, _ in xs:
        send(u0, rx0.at[x], s_x.at[0, d - 1], r_x.at[0, d - 1], at(xx=to))
    rx0[x] = u0[...]
    for d, _, frm in zs:
        arrived(rz1.at[frm], s_red.at[3, d - 1], r_red.at[3, d - 1], at(zz=frm))
    u1[...] = sum([rz1[n] for n in range(1, 8)], rz1[0])
    for d, to, _ in xs:
        send(u1, rx1.at[x], s_x.at[1, d - 1], r_x.at[1, d - 1], at(xx=to))
    rx1[x] = u1[...]
    first_leg(2)

    for d, _, frm in xs:
        arrived(rx0.at[frm], s_x.at[0, d - 1], r_x.at[0, d - 1], at(xx=frm))
    ay0[pl.ds(pl.multiple_of(y * 8, 8), 8), :] = (rx0[0] + rx0[1]) + (rx0[2] + rx0[3])
    mine0 = ay0.at[pl.ds(pl.multiple_of(y * 8, 8), 8), :]
    for d, to, _ in ys:
        send(mine0, mine0, s_red.at[4, d - 1], r_red.at[4, d - 1], at(yy=to))
    for d, _, frm in xs:
        arrived(rx1.at[frm], s_x.at[1, d - 1], r_x.at[1, d - 1], at(xx=frm))
    az1[pl.ds(pl.multiple_of(z * 8, 8), 8), :] = (rx1[0] + rx1[1]) + (rx1[2] + rx1[3])
    mine1 = az1.at[pl.ds(pl.multiple_of(z * 8, 8), 8), :]
    for d, to, _ in zs:
        send(mine1, mine1, s_red.at[5, d - 1], r_red.at[5, d - 1], at(zz=to))

    first_leg(3)
    for d, _, frm in ys:
        arrived(ay0.at[pl.ds(pl.multiple_of(frm * 8, 8), 8), :], s_red.at[4, d - 1], r_red.at[4, d - 1], at(yy=frm))
    az0[z] = ay0[0:40, :]
    for d, to, _ in zs:
        send(ay0.at[0:40, :], az0.at[z], s_red.at[6, d - 1], r_red.at[6, d - 1], at(zz=to))
    for d, _, frm in zs:
        arrived(az1.at[pl.ds(pl.multiple_of(frm * 8, 8), 8), :], s_red.at[5, d - 1], r_red.at[5, d - 1], at(zz=frm))
    ay1[y] = az1[0:40, :]
    for d, to, _ in ys:
        send(az1.at[0:40, :], ay1.at[y], s_red.at[7, d - 1], r_red.at[7, d - 1], at(yy=to))

    for d, _, frm in zs:
        arrived(az0.at[frm], s_red.at[6, d - 1], r_red.at[6, d - 1], at(zz=frm))
    f0[core] = az0[...].reshape(320, 128)
    mine_f0 = f0.at[core]
    send(mine_f0, mine_f0, s_core.at[2], r_core.at[2], at(cc=other))
    for d, _, frm in ys:
        arrived(ay1.at[frm], s_red.at[7, d - 1], r_red.at[7, d - 1], at(yy=frm))
    f1[core] = ay1[...].reshape(320, 128)
    mine_f1 = f1.at[core]
    send(mine_f1, mine_f1, s_core.at[3], r_core.at[3], at(cc=other))

    second_leg()
    arrived(f0.at[other], s_core.at[2], r_core.at[2], at(cc=other))

    def fill(f, blocks):
        for n, (r, c) in enumerate(blocks):
            for part in range(n * 128, n * 128 + 128, 64):
                row = r * 128 + part - n * 128
                S[row:row + 64, c * 128:(c + 1) * 128] = f[part // 320, part % 320:part % 320 + 64, :] * (1.0 / 524288)

    def after_first():
        arrived(f1.at[other], s_core.at[3], r_core.at[3], at(cc=other))
        fill(f1, SECOND)

    def row_copy(n):
        rows = pl.ds(n * 128, 128)
        return pltpu.make_async_copy(upper.at[rows, :], upper_hbm.at[rows, :], out_sem.at[n])

    for r in range(1, 4):
        upper[r * 128:(r + 1) * 128, 0:r * 128] = jnp.zeros((128, r * 128), F32)
    fill(f0, FIRST)
    factor_rows(S, T, upper, after_first, lambda n: row_copy(n).start())
    t0, t1 = T[0].T, T[1].T
    cross = -dot_hi(t0, dot_hi(upper[0:128, 128:256], t1))
    bottom = jnp.concatenate([jnp.zeros((128, 128), F32), t1], axis=1)
    inverse = jnp.concatenate([jnp.concatenate([t0, cross], axis=1), bottom], axis=0)
    pieces[0] = inverse.astype(BF16)
    left = inverse - pieces[0].astype(F32)
    pieces[1] = left.astype(BF16)
    pieces[2] = (left - pieces[1].astype(F32)).astype(BF16)
    pieces_copy = pltpu.make_async_copy(pieces, pieces_hbm, out_sem.at[4])
    pieces_copy.start()
    for d, _, frm in ts:
        arrived(RA2.at[:, frm], s_rel.at[2, d - 1], r_rel.at[2, d - 1], at_t(frm))
    for d, _, frm in zs:
        arrived(RB2.at[frm], s_rel.at[3, d - 1], r_rel.at[3, d - 1], at(zz=frm))

    lead_copies = []
    for n in range(4):
        where = pl.ds(n * 256, 256)
        choose = P_un[where, :]
        lead_out[where, 0:128] = jnp.dot(choose, RA2[...].reshape(2048, 128), preferred_element_type=F32).astype(BF16)
        lead_out[where, 128:256] = jnp.dot(choose, RB2[...].reshape(2048, 128), preferred_element_type=F32).astype(BF16)
        lead_copies.append(pltpu.make_async_copy(lead_out.at[where, :], lead_hbm.at[where, :], out_sem.at[5 + n]))
        lead_copies[n].start()
    for copy in started:
        copy.wait_send()
    for copy in [row_copy(n) for n in range(4)] + [pieces_copy] + lead_copies:
        copy.wait()


def fused(ops, exc, scale, live, ports):
    D = pltpu.SemaphoreType.DMA
    vm = pltpu.VMEM
    H = pl.BlockSpec(memory_space=pl.ANY)
    scratch = [
        vm((2, 512, 1024), BF16), vm((2, 1024, 512), BF16), vm((2, 512, 512), BF16), vm((8, 128, 256), BF16),
        vm((2048, 1024), BF16), vm((1024, 2048), BF16),
        vm((8, 16), I32), pltpu.SMEM((8,), F32), pltpu.SMEM((1,), I32),
        vm((8, 128), F32), vm((8, 8, 128), F32), vm((8, 128), F32), vm((16, 8, 128), F32),
        vm((128, 16, 128), BF16), vm((8, 16, 16, 128), BF16),
        vm((8, 16, 16, 128), BF16), vm((8, 16, 16, 128), BF16), vm((16, 8, 16, 128), BF16), vm((8, 16, 16, 128), BF16),
        vm((512, 512), F32), vm((4, 128, 128), F32), vm((512, 512), F32), vm((3, 256, 256), BF16), vm((1024, 256), BF16), D((9,)),
        vm((640, 128), F32), vm((640, 128), F32), vm((320, 128), F32), vm((320, 128), F32),
        vm((320, 128), F32), vm((320, 128), F32),
        vm((8, 40, 128), F32), vm((8, 40, 128), F32), vm((64, 128), F32), vm((64, 128), F32),
        vm((8, 8, 128), F32), vm((8, 8, 128), F32), vm((8, 128), F32), vm((8, 128), F32),
        vm((4, 8, 128), F32), vm((4, 8, 128), F32),
        vm((64, 128), F32), vm((64, 128), F32), vm((8, 40, 128), F32), vm((8, 40, 128), F32),
        vm((2, 320, 128), F32), vm((2, 320, 128), F32),
        D((7,)), D((2, 3)), D((2, 3)), D((2, 3)), D((2, 3)), D((7,)), D((7,)), D((15,)), D((15,)), D((2, 3)), D((2, 3)),
        D((4,)), D((4,)), D((8, 7)), D((8, 7)), D((2, 3)), D((2, 3)), D((4, 15)), D((4, 15)),
    ]
    out = pl.pallas_call(
        fused_kernel,
        out_shape=tuple(jax.ShapeDtypeStruct(*o) for o in (((512, 512), F32), ((3, 256, 256), BF16), ((1024, 256), BF16))),
        in_specs=[H] * 5, out_specs=(H,) * 3,
        scratch_shapes=scratch,
        compiler_params=pltpu.CompilerParams(collective_id=0, has_side_effects=True, vmem_limit_bytes=62 << 20),
        name="fused",
    )(ops, exc, scale, live, ports)
    return finish(*out)


def solution(mesh):
    placed = (P("comp", "col", None), P("comp", None, "col"), P("comp"), P("comp"), P("comp", "col"))
    return jax.shard_map(fused, mesh=mesh, in_specs=placed, out_specs=(P(("comp", "col"), None, None), P()), check_vma=False)
```

```python
import jax
import jax.numpy as jnp
from jax import lax
from jax.experimental import pallas as pl
from jax.experimental.pallas import tpu as pltpu
from jax.sharding import PartitionSpec as P

MESH = pl.DeviceIdType.MESH
NX, NY, NZ, NT = 4, 8, 8, 16
F32, BF16, I32 = jnp.float32, jnp.bfloat16, jnp.int32
FIRST = [(0, 0), (0, 1), (0, 2), (0, 3), (1, 1)]
SECOND = [(1, 2), (1, 3), (2, 2), (2, 3), (3, 3)]


CUT_Z, CUT_T = (0, 0, 2, 4, 7), (0, 0, 4, 8, 15)
HI = lax.Precision.HIGHEST


def iota(shape, dim):
    return lax.broadcasted_iota(I32, shape, dim)


def dot_hi(a, b, ta=False):
    dims = (((0,), (0,)), ((), ())) if ta else (((1,), (0,)), ((), ()))
    return lax.dot_general(a, b, dims, precision=HI, preferred_element_type=jnp.float32)

def factor_block(S, with_inverse=True):
    sub = lax.broadcasted_iota(jnp.int32, (8, 128), 0)
    lane = lax.broadcasted_iota(jnp.int32, (8, 128), 1)
    S = list(S)
    T = [(lane == sub + 8 * i).astype(jnp.float32) for i in range(16)]
    for j in range(16):
        B = {i: [jnp.broadcast_to(S[i][:, 8 * j + k:8 * j + k + 1], (8, 128)) for k in range(8)] for i in range(j, 16)}
        scale = jnp.zeros((8, 128), jnp.float32)
        for k in range(8):
            piv = B[j][k][k:k + 1, :]
            inv = 1.0 / piv
            scale = jnp.where(sub == k, lax.rsqrt(piv), scale)
            prow, qrow = S[j][k:k + 1, :], T[j][k:k + 1, :]
            brow = [B[j][kk][k:k + 1, :] for kk in range(8)]
            for i in range(j, 16):
                m = B[i][k] * inv
                if i == j:
                    m = jnp.where(sub > k, m, 0.0)
                if i > j or k < 7:
                    S[i] = S[i] - m * prow
                    if with_inverse:
                        T[i] = T[i] - m * qrow
                    for kk in range(k + 1, 8):
                        B[i][kk] = B[i][kk] - m * brow[kk]
        S[j] = jnp.where(lane >= sub + 8 * j, S[j], 0.0) * scale
        T[j] = T[j] * scale
    return S, T


def factor_rows(S, T, upper, after_first, row_done):
    def step(kb, carry):
        r0 = pl.multiple_of(kb * 128, 128)
        U, inverse = factor_block([S[pl.ds(r0 + 8 * i, 8), pl.ds(r0, 128)] for i in range(16)])
        for i in range(16):
            T[kb, 8 * i:8 * i + 8, :] = inverse[i]
            upper[pl.ds(r0 + 8 * i, 8), pl.ds(r0, 128)] = U[i]
        for n in range(3):
            @pl.when(kb == n)
            def _(n=n):
                edge = (n + 1) * 128
                if n == 0:
                    after_first()
                row = dot_hi(T[n], S[n * 128:edge, edge:])
                upper[n * 128:edge, edge:] = row
                row_done(n)
                for r in range(n + 1, 4):
                    right = row[:, r * 128 - edge:]
                    S[r * 128:r * 128 + 128, r * 128:] = S[r * 128:r * 128 + 128, r * 128:] - dot_hi(right[:, 0:128], right, ta=True)
        return carry
    lax.fori_loop(0, 3, step, 0)


def hand_over_kernel(basis_in, upper_in, basis_out, upper_out, basis, upper, sems):
    parts = [(array.at[pl.ds(n * size, size)], middle.at[pl.ds(n * size, size)], out.at[pl.ds(n * size, size)])
             for n in range(4) for array, middle, out, size in ((upper_in, upper, upper_out, 128), (basis_in, basis, basis_out, 32))]
    into = [pltpu.make_async_copy(src, mid, sems.at[0, n]) for n, (src, mid, _) in enumerate(parts)]
    out = [pltpu.make_async_copy(mid, dst, sems.at[1, n]) for n, (_, mid, dst) in enumerate(parts)]
    for copy in into:
        copy.start()
    for first, second in zip(into, out):
        first.wait()
        second.start()
    for copy in out:
        copy.wait()


def hand_over(basis, upper):
    H = pl.BlockSpec(memory_space=pl.ANY)
    return pl.pallas_call(
        hand_over_kernel,
        out_shape=(jax.ShapeDtypeStruct((128, 8, 256), BF16), jax.ShapeDtypeStruct((512, 512), F32)),
        in_specs=[H] * 2, out_specs=(H, H),
        scratch_shapes=[pltpu.VMEM((128, 8, 256), BF16), pltpu.VMEM((512, 512), F32), pltpu.SemaphoreType.DMA((2, 8))],
        compiler_params=pltpu.CompilerParams(vmem_limit_bytes=60 << 20),
        name="hand_over",
    )(basis, upper)


def fused_kernel(ops, exc, scale_hbm, live_hbm, ports_hbm, basis_hbm, upper_hbm,
                 A, E, W, lead, P_pack, P_un, ports, scale, live, pmine, pz, ptile, pall,
                 PA, PB, RA1, RA2, RB1, RB2,
                 S, T, upper, basis, out_sem, g0, g1, r0c, r1c, s0, s1, rz0, ry1, t0, t1, ry0, rz1, u0, u1, rx0, rx1,
                 ay0, az1, az0, ay1, f0, f1,
                 local_sem, s_ops, r_ops, s_exc, r_exc, s_pz, r_pz, s_py, r_py, s_ld, r_ld,
                 s_core, r_core, s_red, r_red, s_x, r_x, s_rel, r_rel):
    comp, x = lax.axis_index("comp"), lax.axis_index("col")
    z, y, core = comp // 16, (comp // 2) % 8, comp % 2
    t = y * 2 + core

    def at(xx=None, yy=None, zz=None, cc=None):
        xx, yy, zz, cc = (x if xx is None else xx, y if yy is None else yy, z if zz is None else zz, core if cc is None else cc)
        return ((zz * 8 + yy) * 2 + cc, xx)

    def at_t(tt):
        return (z * 16 + tt, x)

    started = []

    def send(src, dst, ss, rs, to):
        copy = pltpu.make_async_remote_copy(src_ref=src, dst_ref=dst, send_sem=ss, recv_sem=rs, device_id=to, device_id_type=MESH)
        copy.start()
        started.append(copy)

    def arrived(dst, ss, rs, frm):
        pltpu.make_async_remote_copy(src_ref=dst, dst_ref=dst, send_sem=ss, recv_sem=rs, device_id=frm, device_id_type=MESH).wait_recv()

    xs = [(d, lax.rem(x + d, NX), lax.rem(x + NX - d, NX)) for d in (1, 3, 2)]
    ys = [(d, lax.rem(y + d, NY), lax.rem(y + NY - d, NY)) for d in (4, 3, 5, 2, 6, 1, 7)]
    zs = [(d, lax.rem(z + d, NZ), lax.rem(z + NZ - d, NZ)) for d in (4, 3, 5, 2, 6, 1, 7)]
    ts = [(d, lax.rem(t + d, NT), lax.rem(t + NT - d, NT)) for d in (8, 7, 9, 6, 10, 5, 11, 4, 12, 3, 13, 2, 14, 1, 15)]
    other = 1 - core

    barrier = pltpu.get_barrier_semaphore()
    for _, to, _ in xs:
        pl.semaphore_signal(barrier, inc=1, device_id=at(xx=to), device_id_type=MESH)
    for _, to, _ in zs:
        pl.semaphore_signal(barrier, inc=1, device_id=at(zz=to), device_id_type=MESH)
    for _, to, _ in ts:
        pl.semaphore_signal(barrier, inc=1, device_id=at_t(to), device_id_type=MESH)

    small = [pltpu.make_async_copy(ports_hbm, ports, local_sem.at[4]),
             pltpu.make_async_copy(scale_hbm, scale, local_sem.at[5]),
             pltpu.make_async_copy(live_hbm, live, local_sem.at[6])]
    for copy in small:
        copy.start()
    own = []
    for k in range(2):
        own.append(pltpu.make_async_copy(ops.at[2 * x + k], A.at[k, pl.ds(pl.multiple_of(x * 128, 128), 128), :], local_sem.at[k]))
        own.append(pltpu.make_async_copy(exc.at[2 * x + k], E.at[k, :, pl.ds(pl.multiple_of(x * 128, 128), 128)], local_sem.at[2 + k]))
    for copy in own:
        copy.start()
    pl.semaphore_wait(barrier, 3 + 7 + 15)

    rows_me = pl.ds(pl.multiple_of(x * 128, 128), 128)
    for k in range(2):
        for d, to, _ in xs:
            send(ops.at[2 * to + k], A.at[k, rows_me, :], s_ops.at[k, d - 1], r_ops.at[k, d - 1], at(xx=to))
            send(exc.at[2 * to + k], E.at[k, :, rows_me], s_exc.at[k, d - 1], r_exc.at[k, d - 1], at(xx=to))

    for copy in small:
        copy.wait()
    pick = (iota((16, 128), 1) % 16 == iota((16, 128), 0)).astype(F32).astype(BF16)
    p_high = jnp.dot((ports[...] // 256).astype(F32).astype(BF16), pick, preferred_element_type=F32)
    p_low = jnp.dot((ports[...] % 256).astype(F32).astype(BF16), pick, preferred_element_type=F32)
    p_local = jnp.where(iota((8, 128), 1) // 16 == iota((8, 128), 0), p_high * 256 + p_low, 0.0)
    p_local = jnp.sum(p_local, axis=0, keepdims=True).astype(I32)
    pmine[...] = jnp.broadcast_to(p_local, (8, 128)).astype(F32)
    pz[z] = pmine[...]
    for d, to, _ in zs:
        send(pmine, pz.at[z], s_pz.at[d - 1], r_pz.at[d - 1], at(zz=to))
    target = p_local // 512
    target_all = jnp.broadcast_to(target.astype(F32), (128, 128))
    target_col = target_all.T
    earlier = (target_col == target_all) & (iota((128, 128), 0) < iota((128, 128), 1))
    rank = jnp.sum(earlier.astype(F32), axis=0, keepdims=True)
    base = jnp.broadcast_to(target.astype(F32) * 2 + rank, (8, 128)).astype(BF16)
    spread = (iota((128, 1024), 1) // 8 == iota((128, 1024), 0)).astype(BF16)
    key = jnp.dot(base, spread, preferred_element_type=F32)[0:1, :].astype(I32) * 8 + iota((1, 1024), 1) % 8

    def fill_pack(n, carry):
        P_pack[pl.ds(pl.multiple_of(n * 128, 128), 128), :] = (iota((128, 1024), 0) + n * 128 == key).astype(F32).astype(BF16)
        return carry
    lax.fori_loop(0, 16, fill_pack, 0)

    for d, _, frm in zs:
        arrived(pz.at[frm], s_pz.at[d - 1], r_pz.at[d - 1], at(zz=frm))
    tile = jnp.concatenate([pz[n, 0:1, :] for n in range(8)], axis=0)
    ptile[...] = tile
    pall[t] = tile
    for d, to, _ in ts:
        send(ptile, pall.at[t], s_py.at[d - 1], r_py.at[d - 1], at_t(to))
    for d, _, frm in ts:
        arrived(pall.at[frm], s_py.at[d - 1], r_py.at[d - 1], at_t(frm))
    every = pall[...].reshape(128, 128).astype(I32)
    mine = jnp.where(every // 512 == comp, every % 128 + 1, 0).astype(F32).T
    is_mine = (mine > 0.5)
    below = (iota((128, 128), 1) < iota((128, 128), 0)).astype(BF16)
    order = jnp.dot(below, is_mine.astype(F32).astype(BF16), preferred_element_type=F32)
    zero = jnp.zeros((128, 128), F32)
    first = jnp.sum(jnp.where(is_mine & (order < 0.5), mine, zero), axis=0, keepdims=True)
    second = jnp.sum(jnp.where(is_mine & (order > 0.5), mine, zero), axis=0, keepdims=True)
    both = jnp.concatenate([first, second, jnp.zeros((6, 128), F32)], axis=0).astype(BF16)
    lane = iota((128, 2048), 1) // 16
    widen = ((lane % 16) * 8 + lane // 16 == iota((128, 2048), 0)).astype(F32).astype(BF16)
    wide = jnp.dot(both, widen, preferred_element_type=F32)
    which = (iota((1, 2048), 1) // 8) % 2
    place = jnp.where(which == 0, wide[0:1, :], wide[1:2, :]).astype(I32) * 8 - 8 + iota((1, 2048), 1) % 8

    def fill_un(n, carry):
        P_un[pl.ds(pl.multiple_of(n * 128, 128), 128), :] = (iota((128, 2048), 0) + n * 128 == place).astype(F32).astype(BF16)
        return carry
    lax.fori_loop(0, 8, fill_un, 0)

    def send_leads(k):
        for d, to, _ in xs:
            send(W.at[k, pl.ds(pl.multiple_of(to * 128, 128), 128), pl.ds(0, 256)], lead.at[2 * x + k], s_ld.at[k, d - 1], r_ld.at[k, d - 1], at(xx=to))
        lead[2 * x + k] = W[k, rows_me, 0:256]

    for copy in own:
        copy.wait()
    for k in range(2):
        for d, _, frm in xs:
            there = pl.ds(pl.multiple_of(frm * 128, 128), 128)
            arrived(A.at[k, there, :], s_ops.at[k, d - 1], r_ops.at[k, d - 1], at(xx=frm))
            arrived(E.at[k, :, there], s_exc.at[k, d - 1], r_exc.at[k, d - 1], at(xx=frm))
        slot = 2 * x + k
        alive = jnp.minimum(jnp.maximum(live[0] - slot, 0), 1).astype(F32)
        weight = scale[slot] * alive

        def rows(n, carry):
            where = pl.ds(pl.multiple_of(n * 256, 256), 256)
            product = jnp.dot(A[k, where, :], E[k], preferred_element_type=F32)
            W[k, where, :] = (product * weight).astype(BF16)
            return carry
        lax.fori_loop(0, 2, rows, 0)
        if k == 0:
            send_leads(0)
        for r in range(4):
            out = lax.dot_general(W[k, :, r * 128:(r + 1) * 128], W[k, :, r * 128:], (((0,), (0,)), ((), ())), preferred_element_type=F32)
            for c in range(r, 4):
                g, n = (g0, FIRST.index((r, c))) if (r, c) in FIRST else (g1, SECOND.index((r, c)))
                part = out[:, (c - r) * 128:(c - r + 1) * 128]
                g[n * 128:(n + 1) * 128, :] = part if k == 0 else g[n * 128:(n + 1) * 128, :] + part
            if k == 1 and r == 1:
                send(g0.at[pl.ds(pl.multiple_of(other * 320, 64), 320), :], r0c, s_core.at[0], r_core.at[0], at(cc=other))
    send(g1.at[pl.ds(pl.multiple_of(other * 320, 64), 320), :], r1c, s_core.at[1], r_core.at[1], at(cc=other))
    send_leads(1)
    arrived(r0c, s_core.at[0], r_core.at[0], at(cc=other))
    s0[...] = g0[pl.ds(pl.multiple_of(core * 320, 64), 320), :] + r0c[...]
    for d, to, _ in zs:
        send(s0.at[pl.ds(pl.multiple_of(to * 40, 8), 40), :], rz0.at[z], s_red.at[0, d - 1], r_red.at[0, d - 1], at(zz=to))
    arrived(r1c, s_core.at[1], r_core.at[1], at(cc=other))
    s1[...] = g1[pl.ds(pl.multiple_of(core * 320, 64), 320), :] + r1c[...]
    for d, to, _ in ys:
        send(s1.at[pl.ds(pl.multiple_of(to * 40, 8), 40), :], ry1.at[y], s_red.at[1, d - 1], r_red.at[1, d - 1], at(yy=to))
    rz0[z] = s0[pl.ds(pl.multiple_of(z * 40, 8), 40), :]
    ry1[y] = s1[pl.ds(pl.multiple_of(y * 40, 8), 40), :]

    for k in range(2):
        for d, _, frm in xs:
            arrived(lead.at[2 * frm + k], s_ld.at[k, d - 1], r_ld.at[k, d - 1], at(xx=frm))

    def pack(n, carry):
        packed = jnp.dot(P_pack[pl.ds(pl.multiple_of(n * 256, 256), 256), :], lead[...].reshape(1024, 256), preferred_element_type=F32).astype(BF16)
        PA[pl.ds(n * 16, 16)] = packed[:, 0:128].reshape(16, 16, 128)
        PB[n] = packed[:, 128:256].reshape(16, 16, 128)
        return carry
    lax.fori_loop(0, 8, pack, 0)

    def first_leg(bunch):
        for d, to, _ in zs[CUT_Z[bunch]:CUT_Z[bunch + 1]]:
            send(PA.at[pl.ds(to * 16, 16)], RA1.at[z], s_rel.at[0, d - 1], r_rel.at[0, d - 1], at(zz=to))
        for d, to, _ in ts[CUT_T[bunch]:CUT_T[bunch + 1]]:
            send(PB.at[:, to], RB1.at[t], s_rel.at[1, d - 1], r_rel.at[1, d - 1], at_t(to))

    def second_leg():
        for d, _, frm in zs:
            arrived(RA1.at[frm], s_rel.at[0, d - 1], r_rel.at[0, d - 1], at(zz=frm))
        for d, to, _ in ts:
            send(RA1.at[:, to], RA2.at[:, t], s_rel.at[2, d - 1], r_rel.at[2, d - 1], at_t(to))
        RA2[:, t] = RA1[:, t]
        for d, _, frm in ts:
            arrived(RB1.at[frm], s_rel.at[1, d - 1], r_rel.at[1, d - 1], at_t(frm))
        for d, to, _ in zs:
            send(RB1.at[:, to], RB2.at[z], s_rel.at[3, d - 1], r_rel.at[3, d - 1], at(zz=to))
        RB2[z] = RB1[:, z]

    first_leg(0)
    RA1[z] = PA[pl.ds(z * 16, 16)]
    RB1[t] = PB[:, t]
    for d, _, frm in zs:
        arrived(rz0.at[frm], s_red.at[0, d - 1], r_red.at[0, d - 1], at(zz=frm))
    t0[0:40, :] = sum([rz0[n] for n in range(1, 8)], rz0[0])
    t0[40:64, :] = jnp.zeros((24, 128), F32)
    for d, to, _ in ys:
        send(t0.at[pl.ds(pl.multiple_of(to * 8, 8), 8), :], ry0.at[y], s_red.at[2, d - 1], r_red.at[2, d - 1], at(yy=to))
    ry0[y] = t0[pl.ds(pl.multiple_of(y * 8, 8), 8), :]
    for d, _, frm in ys:
        arrived(ry1.at[frm], s_red.at[1, d - 1], r_red.at[1, d - 1], at(yy=frm))
    t1[0:40, :] = sum([ry1[n] for n in range(1, 8)], ry1[0])
    t1[40:64, :] = jnp.zeros((24, 128), F32)
    for d, to, _ in zs:
        send(t1.at[pl.ds(pl.multiple_of(to * 8, 8), 8), :], rz1.at[z], s_red.at[3, d - 1], r_red.at[3, d - 1], at(zz=to))
    rz1[z] = t1[pl.ds(pl.multiple_of(z * 8, 8), 8), :]

    first_leg(1)
    for d, _, frm in ys:
        arrived(ry0.at[frm], s_red.at[2, d - 1], r_red.at[2, d - 1], at(yy=frm))
    u0[...] = sum([ry0[n] for n in range(1, 8)], ry0[0])
    for d, to, _ in xs:
        send(u0, rx0.at[x], s_x.at[0, d - 1], r_x.at[0, d - 1], at(xx=to))
    rx0[x] = u0[...]
    for d, _, frm in zs:
        arrived(rz1.at[frm], s_red.at[3, d - 1], r_red.at[3, d - 1], at(zz=frm))
    u1[...] = sum([rz1[n] for n in range(1, 8)], rz1[0])
    for d, to, _ in xs:
        send(u1, rx1.at[x], s_x.at[1, d - 1], r_x.at[1, d - 1], at(xx=to))
    rx1[x] = u1[...]
    first_leg(2)

    for d, _, frm in xs:
        arrived(rx0.at[frm], s_x.at[0, d - 1], r_x.at[0, d - 1], at(xx=frm))
    ay0[pl.ds(pl.multiple_of(y * 8, 8), 8), :] = (rx0[0] + rx0[1]) + (rx0[2] + rx0[3])
    mine0 = ay0.at[pl.ds(pl.multiple_of(y * 8, 8), 8), :]
    for d, to, _ in ys:
        send(mine0, mine0, s_red.at[4, d - 1], r_red.at[4, d - 1], at(yy=to))
    for d, _, frm in xs:
        arrived(rx1.at[frm], s_x.at[1, d - 1], r_x.at[1, d - 1], at(xx=frm))
    az1[pl.ds(pl.multiple_of(z * 8, 8), 8), :] = (rx1[0] + rx1[1]) + (rx1[2] + rx1[3])
    mine1 = az1.at[pl.ds(pl.multiple_of(z * 8, 8), 8), :]
    for d, to, _ in zs:
        send(mine1, mine1, s_red.at[5, d - 1], r_red.at[5, d - 1], at(zz=to))

    first_leg(3)
    for d, _, frm in ys:
        arrived(ay0.at[pl.ds(pl.multiple_of(frm * 8, 8), 8), :], s_red.at[4, d - 1], r_red.at[4, d - 1], at(yy=frm))
    az0[z] = ay0[0:40, :]
    for d, to, _ in zs:
        send(ay0.at[0:40, :], az0.at[z], s_red.at[6, d - 1], r_red.at[6, d - 1], at(zz=to))
    for d, _, frm in zs:
        arrived(az1.at[pl.ds(pl.multiple_of(frm * 8, 8), 8), :], s_red.at[5, d - 1], r_red.at[5, d - 1], at(zz=frm))
    ay1[y] = az1[0:40, :]
    for d, to, _ in ys:
        send(az1.at[0:40, :], ay1.at[y], s_red.at[7, d - 1], r_red.at[7, d - 1], at(yy=to))

    for d, _, frm in zs:
        arrived(az0.at[frm], s_red.at[6, d - 1], r_red.at[6, d - 1], at(zz=frm))
    f0[core] = az0[...].reshape(320, 128)
    mine_f0 = f0.at[core]
    send(mine_f0, mine_f0, s_core.at[2], r_core.at[2], at(cc=other))
    for d, _, frm in ys:
        arrived(ay1.at[frm], s_red.at[7, d - 1], r_red.at[7, d - 1], at(yy=frm))
    f1[core] = ay1[...].reshape(320, 128)
    mine_f1 = f1.at[core]
    send(mine_f1, mine_f1, s_core.at[3], r_core.at[3], at(cc=other))

    second_leg()
    arrived(f0.at[other], s_core.at[2], r_core.at[2], at(cc=other))

    def fill(f, blocks):
        for n, (r, c) in enumerate(blocks):
            for part in range(n * 128, n * 128 + 128, 64):
                row = r * 128 + part - n * 128
                S[row:row + 64, c * 128:(c + 1) * 128] = f[part // 320, part % 320:part % 320 + 64, :] * (1.0 / 524288)

    def after_first():
        arrived(f1.at[other], s_core.at[3], r_core.at[3], at(cc=other))
        fill(f1, SECOND)

    def row_copy(n):
        rows = pl.ds(n * 128, 128)
        return pltpu.make_async_copy(upper.at[rows, :], upper_hbm.at[rows, :], out_sem.at[n])

    for r in range(1, 4):
        upper[r * 128:(r + 1) * 128, 0:r * 128] = jnp.zeros((128, r * 128), F32)
    fill(f0, FIRST)
    factor_rows(S, T, upper, after_first, lambda n: row_copy(n).start())
    for d, _, frm in ts:
        arrived(RA2.at[:, frm], s_rel.at[2, d - 1], r_rel.at[2, d - 1], at_t(frm))
    for d, _, frm in zs:
        arrived(RB2.at[frm], s_rel.at[3, d - 1], r_rel.at[3, d - 1], at(zz=frm))

    t0, t1 = T[0].T, T[1].T
    cross = -dot_hi(t0, dot_hi(upper[0:128, 128:256], t1))
    bottom = jnp.concatenate([jnp.zeros((128, 128), F32), t1], axis=1)
    inverse = jnp.concatenate([jnp.concatenate([t0, cross], axis=1), bottom], axis=0)
    high = inverse.astype(BF16)
    left = inverse - high.astype(F32)
    middle = left.astype(BF16)
    low = (left - middle.astype(F32)).astype(BF16)

    def modes(n):
        choose = P_un[n * 256:n * 256 + 256, :]
        one = jnp.dot(choose, RA2[...].reshape(2048, 128), preferred_element_type=F32).astype(BF16)
        two = jnp.dot(choose, RB2[...].reshape(2048, 128), preferred_element_type=F32).astype(BF16)
        block = jnp.concatenate([one, two], axis=1)
        total = jnp.dot(block, low, preferred_element_type=F32)
        total = total + jnp.dot(block, middle, preferred_element_type=F32)
        total = total + jnp.dot(block, high, preferred_element_type=F32)
        basis[n * 32:n * 32 + 32] = total.reshape(32, 8, 256).astype(BF16)
    last, _ = factor_block([S[384 + 8 * i:392 + 8 * i, 384:512] for i in range(16)], False)
    for n in range(4):
        modes(n)
    for i in range(16):
        upper[384 + 8 * i:392 + 8 * i, 384:512] = last[i]
    row_copy(3).start()
    basis_copy = pltpu.make_async_copy(basis, basis_hbm, out_sem.at[4])
    basis_copy.start()
    for copy in started:
        copy.wait_send()
    for copy in [row_copy(n) for n in range(4)] + [basis_copy]:
        copy.wait()


def fused(ops, exc, scale, live, ports):
    D = pltpu.SemaphoreType.DMA
    vm = pltpu.VMEM
    H = pl.BlockSpec(memory_space=pl.ANY)
    scratch = [
        vm((2, 512, 1024), BF16), vm((2, 1024, 512), BF16), vm((2, 512, 512), BF16), vm((8, 128, 256), BF16),
        vm((2048, 1024), BF16), vm((1024, 2048), BF16),
        vm((8, 16), I32), pltpu.SMEM((8,), F32), pltpu.SMEM((1,), I32),
        vm((8, 128), F32), vm((8, 8, 128), F32), vm((8, 128), F32), vm((16, 8, 128), F32),
        vm((128, 16, 128), BF16), vm((8, 16, 16, 128), BF16),
        vm((8, 16, 16, 128), BF16), vm((8, 16, 16, 128), BF16), vm((16, 8, 16, 128), BF16), vm((8, 16, 16, 128), BF16),
        vm((512, 512), F32), vm((4, 128, 128), F32), vm((512, 512), F32), vm((128, 8, 256), BF16), D((5,)),
        vm((640, 128), F32), vm((640, 128), F32), vm((320, 128), F32), vm((320, 128), F32),
        vm((320, 128), F32), vm((320, 128), F32),
        vm((8, 40, 128), F32), vm((8, 40, 128), F32), vm((64, 128), F32), vm((64, 128), F32),
        vm((8, 8, 128), F32), vm((8, 8, 128), F32), vm((8, 128), F32), vm((8, 128), F32),
        vm((4, 8, 128), F32), vm((4, 8, 128), F32),
        vm((64, 128), F32), vm((64, 128), F32), vm((8, 40, 128), F32), vm((8, 40, 128), F32),
        vm((2, 320, 128), F32), vm((2, 320, 128), F32),
        D((7,)), D((2, 3)), D((2, 3)), D((2, 3)), D((2, 3)), D((7,)), D((7,)), D((15,)), D((15,)), D((2, 3)), D((2, 3)),
        D((4,)), D((4,)), D((8, 7)), D((8, 7)), D((2, 3)), D((2, 3)), D((4, 15)), D((4, 15)),
    ]
    out = pl.pallas_call(
        fused_kernel,
        out_shape=tuple(jax.ShapeDtypeStruct(*o) for o in (((128, 8, 256), BF16), ((512, 512), F32))),
        in_specs=[H] * 5, out_specs=(H,) * 2,
        scratch_shapes=scratch,
        compiler_params=pltpu.CompilerParams(collective_id=0, has_side_effects=True, vmem_limit_bytes=62 << 20),
        name="fused",
    )(ops, exc, scale, live, ports)
    return hand_over(*out)


def solution(mesh):
    placed = (P("comp", "col", None), P("comp", None, "col"), P("comp"), P("comp"), P("comp", "col"))
    return jax.shard_map(fused, mesh=mesh, in_specs=placed, out_specs=(P(("comp", "col"), None, None), P()), check_vma=False)
```

```python
import jax
import jax.numpy as jnp
from jax import lax
from jax.experimental import pallas as pl
from jax.experimental.pallas import tpu as pltpu
from jax.sharding import PartitionSpec as P

MESH = pl.DeviceIdType.MESH
NX, NY, NZ, NT = 4, 8, 8, 16
F32, BF16, I32 = jnp.float32, jnp.bfloat16, jnp.int32
FIRST = [(0, 0), (0, 1), (0, 2), (0, 3), (1, 1)]
SECOND = [(1, 2), (1, 3), (2, 2), (2, 3), (3, 3)]


CUT_Z, CUT_T = (0, 0, 2, 4, 7), (0, 0, 4, 8, 15)
HI = lax.Precision.HIGHEST


def iota(shape, dim):
    return lax.broadcasted_iota(I32, shape, dim)


def dot_hi(a, b, ta=False):
    dims = (((0,), (0,)), ((), ())) if ta else (((1,), (0,)), ((), ()))
    return lax.dot_general(a, b, dims, precision=HI, preferred_element_type=jnp.float32)

def factor_block(S, with_inverse=True):
    sub = lax.broadcasted_iota(jnp.int32, (8, 128), 0)
    lane = lax.broadcasted_iota(jnp.int32, (8, 128), 1)
    S = list(S)
    T = [(lane == sub + 8 * i).astype(jnp.float32) for i in range(16)]
    for j in range(16):
        rows = range(j, 8 if j < 8 else 16)
        B = {i: [jnp.broadcast_to(S[i][:, 8 * j + k:8 * j + k + 1], (8, 128)) for k in range(8)] for i in rows}
        scale = jnp.zeros((8, 128), jnp.float32)
        for k in range(8):
            piv = B[j][k][k:k + 1, :]
            inv = 1.0 / piv
            scale = jnp.where(sub == k, lax.rsqrt(piv), scale)
            prow, qrow = S[j][k:k + 1, :], T[j][k:k + 1, :]
            brow = [B[j][kk][k:k + 1, :] for kk in range(8)]
            for i in rows:
                m = B[i][k] * inv
                if i == j:
                    m = jnp.where(sub > k, m, 0.0)
                if i > j or k < 7:
                    S[i] = S[i] - m * prow
                    if with_inverse:
                        T[i] = T[i] - m * qrow
                    for kk in range(k + 1, 8):
                        B[i][kk] = B[i][kk] - m * brow[kk]
        S[j] = jnp.where(lane >= sub + 8 * j, S[j], 0.0) * scale
        T[j] = T[j] * scale
        if j == 7:
            top = jnp.concatenate(S[0:8], axis=0)
            change = dot_hi(top, jnp.concatenate([top, jnp.concatenate(T[0:8], axis=0)], axis=1) if with_inverse else top, ta=True)
            for i in range(8, 16):
                S[i] = S[i] - change[8 * i:8 * i + 8, 0:128]
                if with_inverse:
                    T[i] = T[i] - change[8 * i:8 * i + 8, 128:256]
    return S, T


def factor_rows(S, T, upper, after_first, row_done):
    def step(kb, carry):
        r0 = pl.multiple_of(kb * 128, 128)
        U, inverse = factor_block([S[pl.ds(r0 + 8 * i, 8), pl.ds(r0, 128)] for i in range(16)])
        for i in range(16):
            T[kb, 8 * i:8 * i + 8, :] = inverse[i]
            upper[pl.ds(r0 + 8 * i, 8), pl.ds(r0, 128)] = U[i]
        for n in range(3):
            @pl.when(kb == n)
            def _(n=n):
                edge = (n + 1) * 128
                if n == 0:
                    after_first()
                row = dot_hi(T[n], S[n * 128:edge, edge:])
                upper[n * 128:edge, edge:] = row
                row_done(n)
                for r in range(n + 1, 4):
                    right = row[:, r * 128 - edge:]
                    S[r * 128:r * 128 + 128, r * 128:] = S[r * 128:r * 128 + 128, r * 128:] - dot_hi(right[:, 0:128], right, ta=True)
        return carry
    lax.fori_loop(0, 3, step, 0)


def hand_over_kernel(basis_in, upper_in, basis_out, upper_out, basis, upper, sems):
    parts = [(array.at[pl.ds(n * size, size)], middle.at[pl.ds(n * size, size)], out.at[pl.ds(n * size, size)])
             for n in range(4) for array, middle, out, size in ((upper_in, upper, upper_out, 128), (basis_in, basis, basis_out, 32))]
    into = [pltpu.make_async_copy(src, mid, sems.at[0, n]) for n, (src, mid, _) in enumerate(parts)]
    out = [pltpu.make_async_copy(mid, dst, sems.at[1, n]) for n, (_, mid, dst) in enumerate(parts)]
    for copy in into:
        copy.start()
    for first, second in zip(into, out):
        first.wait()
        second.start()
    for copy in out:
        copy.wait()


def hand_over(basis, upper):
    H = pl.BlockSpec(memory_space=pl.ANY)
    return pl.pallas_call(
        hand_over_kernel,
        out_shape=(jax.ShapeDtypeStruct((128, 8, 256), BF16), jax.ShapeDtypeStruct((512, 512), F32)),
        in_specs=[H] * 2, out_specs=(H, H),
        scratch_shapes=[pltpu.VMEM((128, 8, 256), BF16), pltpu.VMEM((512, 512), F32), pltpu.SemaphoreType.DMA((2, 8))],
        compiler_params=pltpu.CompilerParams(vmem_limit_bytes=60 << 20),
        name="hand_over",
    )(basis, upper)


def fused_kernel(ops, exc, scale_hbm, live_hbm, ports_hbm, basis_hbm, upper_hbm,
                 A, E, W, lead, P_pack, P_un, ports, scale, live, pmine, pz, ptile, pall,
                 PA, PB, RA1, RA2, RB1, RB2,
                 S, T, upper, basis, out_sem, g0, g1, r0c, r1c, s0, s1, rz0, ry1, t0, t1, ry0, rz1, u0, u1, rx0, rx1,
                 ay0, az1, az0, ay1, f0, f1,
                 local_sem, s_ops, r_ops, s_exc, r_exc, s_pz, r_pz, s_py, r_py, s_ld, r_ld,
                 s_core, r_core, s_red, r_red, s_x, r_x, s_rel, r_rel):
    comp, x = lax.axis_index("comp"), lax.axis_index("col")
    z, y, core = comp // 16, (comp // 2) % 8, comp % 2
    t = y * 2 + core

    def at(xx=None, yy=None, zz=None, cc=None):
        xx, yy, zz, cc = (x if xx is None else xx, y if yy is None else yy, z if zz is None else zz, core if cc is None else cc)
        return ((zz * 8 + yy) * 2 + cc, xx)

    def at_t(tt):
        return (z * 16 + tt, x)

    started = []

    def send(src, dst, ss, rs, to):
        copy = pltpu.make_async_remote_copy(src_ref=src, dst_ref=dst, send_sem=ss, recv_sem=rs, device_id=to, device_id_type=MESH)
        copy.start()
        started.append(copy)

    def arrived(dst, ss, rs, frm):
        pltpu.make_async_remote_copy(src_ref=dst, dst_ref=dst, send_sem=ss, recv_sem=rs, device_id=frm, device_id_type=MESH).wait_recv()

    xs = [(d, lax.rem(x + d, NX), lax.rem(x + NX - d, NX)) for d in (1, 3, 2)]
    ys = [(d, lax.rem(y + d, NY), lax.rem(y + NY - d, NY)) for d in (4, 3, 5, 2, 6, 1, 7)]
    zs = [(d, lax.rem(z + d, NZ), lax.rem(z + NZ - d, NZ)) for d in (4, 3, 5, 2, 6, 1, 7)]
    ts = [(d, lax.rem(t + d, NT), lax.rem(t + NT - d, NT)) for d in (8, 7, 9, 6, 10, 5, 11, 4, 12, 3, 13, 2, 14, 1, 15)]
    other = 1 - core

    barrier = pltpu.get_barrier_semaphore()
    for _, to, _ in xs:
        pl.semaphore_signal(barrier, inc=1, device_id=at(xx=to), device_id_type=MESH)
    for _, to, _ in zs:
        pl.semaphore_signal(barrier, inc=1, device_id=at(zz=to), device_id_type=MESH)
    for _, to, _ in ts:
        pl.semaphore_signal(barrier, inc=1, device_id=at_t(to), device_id_type=MESH)

    small = [pltpu.make_async_copy(ports_hbm, ports, local_sem.at[4]),
             pltpu.make_async_copy(scale_hbm, scale, local_sem.at[5]),
             pltpu.make_async_copy(live_hbm, live, local_sem.at[6])]
    for copy in small:
        copy.start()
    own = []
    for k in range(2):
        own.append(pltpu.make_async_copy(ops.at[2 * x + k], A.at[k, pl.ds(pl.multiple_of(x * 128, 128), 128), :], local_sem.at[k]))
        own.append(pltpu.make_async_copy(exc.at[2 * x + k], E.at[k, :, pl.ds(pl.multiple_of(x * 128, 128), 128)], local_sem.at[2 + k]))
    for copy in own:
        copy.start()
    pl.semaphore_wait(barrier, 3 + 7 + 15)

    rows_me = pl.ds(pl.multiple_of(x * 128, 128), 128)
    for k in range(2):
        for d, to, _ in xs:
            send(ops.at[2 * to + k], A.at[k, rows_me, :], s_ops.at[k, d - 1], r_ops.at[k, d - 1], at(xx=to))
            send(exc.at[2 * to + k], E.at[k, :, rows_me], s_exc.at[k, d - 1], r_exc.at[k, d - 1], at(xx=to))

    for copy in small:
        copy.wait()
    pick = (iota((16, 128), 1) % 16 == iota((16, 128), 0)).astype(F32).astype(BF16)
    p_high = jnp.dot((ports[...] // 256).astype(F32).astype(BF16), pick, preferred_element_type=F32)
    p_low = jnp.dot((ports[...] % 256).astype(F32).astype(BF16), pick, preferred_element_type=F32)
    p_local = jnp.where(iota((8, 128), 1) // 16 == iota((8, 128), 0), p_high * 256 + p_low, 0.0)
    p_local = jnp.sum(p_local, axis=0, keepdims=True).astype(I32)
    pmine[...] = jnp.broadcast_to(p_local, (8, 128)).astype(F32)
    pz[z] = pmine[...]
    for d, to, _ in zs:
        send(pmine, pz.at[z], s_pz.at[d - 1], r_pz.at[d - 1], at(zz=to))
    target = p_local // 512
    target_all = jnp.broadcast_to(target.astype(F32), (128, 128))
    target_col = target_all.T
    earlier = (target_col == target_all) & (iota((128, 128), 0) < iota((128, 128), 1))
    rank = jnp.sum(earlier.astype(F32), axis=0, keepdims=True)
    base = jnp.broadcast_to(target.astype(F32) * 2 + rank, (8, 128)).astype(BF16)
    spread = (iota((128, 1024), 1) // 8 == iota((128, 1024), 0)).astype(BF16)
    key = jnp.dot(base, spread, preferred_element_type=F32)[0:1, :].astype(I32) * 8 + iota((1, 1024), 1) % 8

    def fill_pack(n, carry):
        P_pack[pl.ds(pl.multiple_of(n * 128, 128), 128), :] = (iota((128, 1024), 0) + n * 128 == key).astype(F32).astype(BF16)
        return carry
    lax.fori_loop(0, 16, fill_pack, 0)

    for d, _, frm in zs:
        arrived(pz.at[frm], s_pz.at[d - 1], r_pz.at[d - 1], at(zz=frm))
    tile = jnp.concatenate([pz[n, 0:1, :] for n in range(8)], axis=0)
    ptile[...] = tile
    pall[t] = tile
    for d, to, _ in ts:
        send(ptile, pall.at[t], s_py.at[d - 1], r_py.at[d - 1], at_t(to))
    for d, _, frm in ts:
        arrived(pall.at[frm], s_py.at[d - 1], r_py.at[d - 1], at_t(frm))
    every = pall[...].reshape(128, 128).astype(I32)
    mine = jnp.where(every // 512 == comp, every % 128 + 1, 0).astype(F32).T
    is_mine = (mine > 0.5)
    below = (iota((128, 128), 1) < iota((128, 128), 0)).astype(BF16)
    order = jnp.dot(below, is_mine.astype(F32).astype(BF16), preferred_element_type=F32)
    zero = jnp.zeros((128, 128), F32)
    first = jnp.sum(jnp.where(is_mine & (order < 0.5), mine, zero), axis=0, keepdims=True)
    second = jnp.sum(jnp.where(is_mine & (order > 0.5), mine, zero), axis=0, keepdims=True)
    both = jnp.concatenate([first, second, jnp.zeros((6, 128), F32)], axis=0).astype(BF16)
    lane = iota((128, 2048), 1) // 16
    widen = ((lane % 16) * 8 + lane // 16 == iota((128, 2048), 0)).astype(F32).astype(BF16)
    wide = jnp.dot(both, widen, preferred_element_type=F32)
    which = (iota((1, 2048), 1) // 8) % 2
    place = jnp.where(which == 0, wide[0:1, :], wide[1:2, :]).astype(I32) * 8 - 8 + iota((1, 2048), 1) % 8

    def fill_un(n, carry):
        P_un[pl.ds(pl.multiple_of(n * 128, 128), 128), :] = (iota((128, 2048), 0) + n * 128 == place).astype(F32).astype(BF16)
        return carry
    lax.fori_loop(0, 8, fill_un, 0)

    def send_leads(k):
        for d, to, _ in xs:
            send(W.at[k, pl.ds(pl.multiple_of(to * 128, 128), 128), pl.ds(0, 256)], lead.at[2 * x + k], s_ld.at[k, d - 1], r_ld.at[k, d - 1], at(xx=to))
        lead[2 * x + k] = W[k, rows_me, 0:256]

    for copy in own:
        copy.wait()
    for k in range(2):
        for d, _, frm in xs:
            there = pl.ds(pl.multiple_of(frm * 128, 128), 128)
            arrived(A.at[k, there, :], s_ops.at[k, d - 1], r_ops.at[k, d - 1], at(xx=frm))
            arrived(E.at[k, :, there], s_exc.at[k, d - 1], r_exc.at[k, d - 1], at(xx=frm))
        slot = 2 * x + k
        alive = jnp.minimum(jnp.maximum(live[0] - slot, 0), 1).astype(F32)
        weight = scale[slot] * alive

        def rows(n, carry):
            where = pl.ds(pl.multiple_of(n * 256, 256), 256)
            product = jnp.dot(A[k, where, :], E[k], preferred_element_type=F32)
            W[k, where, :] = (product * weight).astype(BF16)
            return carry
        lax.fori_loop(0, 2, rows, 0)
        send_leads(k)
        for r in range(4):
            out = lax.dot_general(W[k, :, r * 128:(r + 1) * 128], W[k, :, r * 128:], (((0,), (0,)), ((), ())), preferred_element_type=F32)
            for c in range(r, 4):
                g, n = (g0, FIRST.index((r, c))) if (r, c) in FIRST else (g1, SECOND.index((r, c)))
                part = out[:, (c - r) * 128:(c - r + 1) * 128]
                g[n * 128:(n + 1) * 128, :] = part if k == 0 else g[n * 128:(n + 1) * 128, :] + part
            if k == 1 and r == 1:
                send(g0.at[pl.ds(pl.multiple_of(other * 320, 64), 320), :], r0c, s_core.at[0], r_core.at[0], at(cc=other))
    send(g1.at[pl.ds(pl.multiple_of(other * 320, 64), 320), :], r1c, s_core.at[1], r_core.at[1], at(cc=other))
    arrived(r0c, s_core.at[0], r_core.at[0], at(cc=other))
    s0[...] = g0[pl.ds(pl.multiple_of(core * 320, 64), 320), :] + r0c[...]
    for d, to, _ in zs:
        send(s0.at[pl.ds(pl.multiple_of(to * 40, 8), 40), :], rz0.at[z], s_red.at[0, d - 1], r_red.at[0, d - 1], at(zz=to))
    arrived(r1c, s_core.at[1], r_core.at[1], at(cc=other))
    s1[...] = g1[pl.ds(pl.multiple_of(core * 320, 64), 320), :] + r1c[...]
    for d, to, _ in ys:
        send(s1.at[pl.ds(pl.multiple_of(to * 40, 8), 40), :], ry1.at[y], s_red.at[1, d - 1], r_red.at[1, d - 1], at(yy=to))
    rz0[z] = s0[pl.ds(pl.multiple_of(z * 40, 8), 40), :]
    ry1[y] = s1[pl.ds(pl.multiple_of(y * 40, 8), 40), :]

    for k in range(2):
        for d, _, frm in xs:
            arrived(lead.at[2 * frm + k], s_ld.at[k, d - 1], r_ld.at[k, d - 1], at(xx=frm))

    def pack(n, carry):
        packed = jnp.dot(P_pack[pl.ds(pl.multiple_of(n * 256, 256), 256), :], lead[...].reshape(1024, 256), preferred_element_type=F32).astype(BF16)
        PA[pl.ds(n * 16, 16)] = packed[:, 0:128].reshape(16, 16, 128)
        PB[n] = packed[:, 128:256].reshape(16, 16, 128)
        return carry
    lax.fori_loop(0, 8, pack, 0)

    def first_leg(bunch):
        for d, to, _ in zs[CUT_Z[bunch]:CUT_Z[bunch + 1]]:
            send(PA.at[pl.ds(to * 16, 16)], RA1.at[z], s_rel.at[0, d - 1], r_rel.at[0, d - 1], at(zz=to))
        for d, to, _ in ts[CUT_T[bunch]:CUT_T[bunch + 1]]:
            send(PB.at[:, to], RB1.at[t], s_rel.at[1, d - 1], r_rel.at[1, d - 1], at_t(to))

    def second_leg():
        for d, _, frm in zs:
            arrived(RA1.at[frm], s_rel.at[0, d - 1], r_rel.at[0, d - 1], at(zz=frm))
        for d, to, _ in ts:
            send(RA1.at[:, to], RA2.at[:, t], s_rel.at[2, d - 1], r_rel.at[2, d - 1], at_t(to))
        RA2[:, t] = RA1[:, t]
        for d, _, frm in ts:
            arrived(RB1.at[frm], s_rel.at[1, d - 1], r_rel.at[1, d - 1], at_t(frm))
        for d, to, _ in zs:
            send(RB1.at[:, to], RB2.at[z], s_rel.at[3, d - 1], r_rel.at[3, d - 1], at(zz=to))
        RB2[z] = RB1[:, z]

    first_leg(0)
    RA1[z] = PA[pl.ds(z * 16, 16)]
    RB1[t] = PB[:, t]
    for d, _, frm in zs:
        arrived(rz0.at[frm], s_red.at[0, d - 1], r_red.at[0, d - 1], at(zz=frm))
    t0[0:40, :] = sum([rz0[n] for n in range(1, 8)], rz0[0])
    t0[40:64, :] = jnp.zeros((24, 128), F32)
    for d, to, _ in ys:
        send(t0.at[pl.ds(pl.multiple_of(to * 8, 8), 8), :], ry0.at[y], s_red.at[2, d - 1], r_red.at[2, d - 1], at(yy=to))
    ry0[y] = t0[pl.ds(pl.multiple_of(y * 8, 8), 8), :]
    for d, _, frm in ys:
        arrived(ry1.at[frm], s_red.at[1, d - 1], r_red.at[1, d - 1], at(yy=frm))
    t1[0:40, :] = sum([ry1[n] for n in range(1, 8)], ry1[0])
    t1[40:64, :] = jnp.zeros((24, 128), F32)
    for d, to, _ in zs:
        send(t1.at[pl.ds(pl.multiple_of(to * 8, 8), 8), :], rz1.at[z], s_red.at[3, d - 1], r_red.at[3, d - 1], at(zz=to))
    rz1[z] = t1[pl.ds(pl.multiple_of(z * 8, 8), 8), :]

    first_leg(1)
    for d, _, frm in ys:
        arrived(ry0.at[frm], s_red.at[2, d - 1], r_red.at[2, d - 1], at(yy=frm))
    u0[...] = sum([ry0[n] for n in range(1, 8)], ry0[0])
    for d, to, _ in xs:
        send(u0, rx0.at[x], s_x.at[0, d - 1], r_x.at[0, d - 1], at(xx=to))
    rx0[x] = u0[...]
    for d, _, frm in zs:
        arrived(rz1.at[frm], s_red.at[3, d - 1], r_red.at[3, d - 1], at(zz=frm))
    u1[...] = sum([rz1[n] for n in range(1, 8)], rz1[0])
    for d, to, _ in xs:
        send(u1, rx1.at[x], s_x.at[1, d - 1], r_x.at[1, d - 1], at(xx=to))
    rx1[x] = u1[...]
    first_leg(2)

    for d, _, frm in xs:
        arrived(rx0.at[frm], s_x.at[0, d - 1], r_x.at[0, d - 1], at(xx=frm))
    ay0[pl.ds(pl.multiple_of(y * 8, 8), 8), :] = (rx0[0] + rx0[1]) + (rx0[2] + rx0[3])
    mine0 = ay0.at[pl.ds(pl.multiple_of(y * 8, 8), 8), :]
    for d, to, _ in ys:
        send(mine0, mine0, s_red.at[4, d - 1], r_red.at[4, d - 1], at(yy=to))
    for d, _, frm in xs:
        arrived(rx1.at[frm], s_x.at[1, d - 1], r_x.at[1, d - 1], at(xx=frm))
    az1[pl.ds(pl.multiple_of(z * 8, 8), 8), :] = (rx1[0] + rx1[1]) + (rx1[2] + rx1[3])
    mine1 = az1.at[pl.ds(pl.multiple_of(z * 8, 8), 8), :]
    for d, to, _ in zs:
        send(mine1, mine1, s_red.at[5, d - 1], r_red.at[5, d - 1], at(zz=to))

    first_leg(3)
    for d, _, frm in ys:
        arrived(ay0.at[pl.ds(pl.multiple_of(frm * 8, 8), 8), :], s_red.at[4, d - 1], r_red.at[4, d - 1], at(yy=frm))
    az0[z] = ay0[0:40, :]
    for d, to, _ in zs:
        send(ay0.at[0:40, :], az0.at[z], s_red.at[6, d - 1], r_red.at[6, d - 1], at(zz=to))
    for d, _, frm in zs:
        arrived(az1.at[pl.ds(pl.multiple_of(frm * 8, 8), 8), :], s_red.at[5, d - 1], r_red.at[5, d - 1], at(zz=frm))
    ay1[y] = az1[0:40, :]
    for d, to, _ in ys:
        send(az1.at[0:40, :], ay1.at[y], s_red.at[7, d - 1], r_red.at[7, d - 1], at(yy=to))

    for d, _, frm in zs:
        arrived(az0.at[frm], s_red.at[6, d - 1], r_red.at[6, d - 1], at(zz=frm))
    f0[core] = az0[...].reshape(320, 128)
    mine_f0 = f0.at[core]
    send(mine_f0, mine_f0, s_core.at[2], r_core.at[2], at(cc=other))
    for d, _, frm in ys:
        arrived(ay1.at[frm], s_red.at[7, d - 1], r_red.at[7, d - 1], at(yy=frm))
    f1[core] = ay1[...].reshape(320, 128)
    mine_f1 = f1.at[core]
    send(mine_f1, mine_f1, s_core.at[3], r_core.at[3], at(cc=other))

    second_leg()
    arrived(f0.at[other], s_core.at[2], r_core.at[2], at(cc=other))

    def fill(f, blocks):
        for n, (r, c) in enumerate(blocks):
            for part in range(n * 128, n * 128 + 128, 64):
                row = r * 128 + part - n * 128
                S[row:row + 64, c * 128:(c + 1) * 128] = f[part // 320, part % 320:part % 320 + 64, :] * (1.0 / 524288)

    def after_first():
        arrived(f1.at[other], s_core.at[3], r_core.at[3], at(cc=other))
        fill(f1, SECOND)

    def row_copy(n):
        rows = pl.ds(n * 128, 128)
        return pltpu.make_async_copy(upper.at[rows, :], upper_hbm.at[rows, :], out_sem.at[n])

    for r in range(1, 4):
        upper[r * 128:(r + 1) * 128, 0:r * 128] = jnp.zeros((128, r * 128), F32)
    fill(f0, FIRST)
    factor_rows(S, T, upper, after_first, lambda n: row_copy(n).start())
    for d, _, frm in ts:
        arrived(RA2.at[:, frm], s_rel.at[2, d - 1], r_rel.at[2, d - 1], at_t(frm))
    for d, _, frm in zs:
        arrived(RB2.at[frm], s_rel.at[3, d - 1], r_rel.at[3, d - 1], at(zz=frm))

    t0, t1 = T[0].T, T[1].T
    cross = -dot_hi(t0, dot_hi(upper[0:128, 128:256], t1))
    bottom = jnp.concatenate([jnp.zeros((128, 128), F32), t1], axis=1)
    inverse = jnp.concatenate([jnp.concatenate([t0, cross], axis=1), bottom], axis=0)
    high = inverse.astype(BF16)
    left = inverse - high.astype(F32)
    middle = left.astype(BF16)
    low = (left - middle.astype(F32)).astype(BF16)

    def modes(n):
        choose = P_un[n * 256:n * 256 + 256, :]
        one = jnp.dot(choose, RA2[...].reshape(2048, 128), preferred_element_type=F32).astype(BF16)
        two = jnp.dot(choose, RB2[...].reshape(2048, 128), preferred_element_type=F32).astype(BF16)
        block = jnp.concatenate([one, two], axis=1)
        total = jnp.dot(block, low, preferred_element_type=F32)
        total = total + jnp.dot(block, middle, preferred_element_type=F32)
        total = total + jnp.dot(block, high, preferred_element_type=F32)
        basis[n * 32:n * 32 + 32] = total.reshape(32, 8, 256).astype(BF16)
    last, _ = factor_block([S[384 + 8 * i:392 + 8 * i, 384:512] for i in range(16)], False)
    for n in range(4):
        modes(n)
    for i in range(16):
        upper[384 + 8 * i:392 + 8 * i, 384:512] = last[i]
    row_copy(3).start()
    basis_copy = pltpu.make_async_copy(basis, basis_hbm, out_sem.at[4])
    basis_copy.start()
    for copy in started:
        copy.wait_send()
    for copy in [row_copy(n) for n in range(4)] + [basis_copy]:
        copy.wait()


def fused(ops, exc, scale, live, ports):
    D = pltpu.SemaphoreType.DMA
    vm = pltpu.VMEM
    H = pl.BlockSpec(memory_space=pl.ANY)
    scratch = [
        vm((2, 512, 1024), BF16), vm((2, 1024, 512), BF16), vm((2, 512, 512), BF16), vm((8, 128, 256), BF16),
        vm((2048, 1024), BF16), vm((1024, 2048), BF16),
        vm((8, 16), I32), pltpu.SMEM((8,), F32), pltpu.SMEM((1,), I32),
        vm((8, 128), F32), vm((8, 8, 128), F32), vm((8, 128), F32), vm((16, 8, 128), F32),
        vm((128, 16, 128), BF16), vm((8, 16, 16, 128), BF16),
        vm((8, 16, 16, 128), BF16), vm((8, 16, 16, 128), BF16), vm((16, 8, 16, 128), BF16), vm((8, 16, 16, 128), BF16),
        vm((512, 512), F32), vm((4, 128, 128), F32), vm((512, 512), F32), vm((128, 8, 256), BF16), D((5,)),
        vm((640, 128), F32), vm((640, 128), F32), vm((320, 128), F32), vm((320, 128), F32),
        vm((320, 128), F32), vm((320, 128), F32),
        vm((8, 40, 128), F32), vm((8, 40, 128), F32), vm((64, 128), F32), vm((64, 128), F32),
        vm((8, 8, 128), F32), vm((8, 8, 128), F32), vm((8, 128), F32), vm((8, 128), F32),
        vm((4, 8, 128), F32), vm((4, 8, 128), F32),
        vm((64, 128), F32), vm((64, 128), F32), vm((8, 40, 128), F32), vm((8, 40, 128), F32),
        vm((2, 320, 128), F32), vm((2, 320, 128), F32),
        D((7,)), D((2, 3)), D((2, 3)), D((2, 3)), D((2, 3)), D((7,)), D((7,)), D((15,)), D((15,)), D((2, 3)), D((2, 3)),
        D((4,)), D((4,)), D((8, 7)), D((8, 7)), D((2, 3)), D((2, 3)), D((4, 15)), D((4, 15)),
    ]
    out = pl.pallas_call(
        fused_kernel,
        out_shape=tuple(jax.ShapeDtypeStruct(*o) for o in (((128, 8, 256), BF16), ((512, 512), F32))),
        in_specs=[H] * 5, out_specs=(H,) * 2,
        scratch_shapes=scratch,
        compiler_params=pltpu.CompilerParams(collective_id=0, has_side_effects=True, vmem_limit_bytes=62 << 20),
        name="fused",
    )(ops, exc, scale, live, ports)
    return hand_over(*out)


def solution(mesh):
    placed = (P("comp", "col", None), P("comp", None, "col"), P("comp"), P("comp"), P("comp", "col"))
    return jax.shard_map(fused, mesh=mesh, in_specs=placed, out_specs=(P(("comp", "col"), None, None), P()), check_vma=False)
```
